32 devices in a mesh: dp: 16 (over z, x, core), head: 2 (over y).
Axes of the slice: x: 2, y: 2, z: 4, core: 2. Of those that a mesh axis runs over, the one named last changes fastest.
Arguments:
- tokens: bfloat16 [16384, 768], P(('dp', 'head')), may hold values from -6 to 6
- segments: int32 [16384], P('dp'), may hold values from 0 to 2, as said below
- padding: int32 [16384], P('dp'), may hold values from 0 to 1, as said below
- cotangent: bfloat16 [16384, 768], P(('dp', 'head')), may hold values from -6 to 6
- gain_one: float32 [768], replicated, may hold values from 0.5 to 1.5
- shift_one: float32 [768], replicated, may hold values from -2 to 2
- w_query: bfloat16 [768, 768], P(None, 'head'), may hold values from -0.3125 to 0.3125
- b_query: float32 [768], P('head'), may hold values from -3 to 3
- w_key: bfloat16 [768, 768], P(None, 'head'), may hold values from -0.3125 to 0.3125
- w_value: bfloat16 [768, 768], P(None, 'head'), may hold values from -0.21875 to 0.21875
- b_value: float32 [768], P('head'), may hold values from -3 to 3
- w_out: bfloat16 [768, 768], P('head'), may hold values from -0.625 to 0.625
- b_out: float32 [768], replicated, may hold values from -2 to 2
- gain_two: float32 [768], replicated, may hold values from 0.5 to 1.5
- shift_two: float32 [768], replicated, may hold values from -2 to 2
- w_up: bfloat16 [768, 3072], P(None, 'head'), may hold values from -0.21875 to 0.21875
- b_up: float32 [3072], replicated, may hold values from -2 to 2
- w_down: bfloat16 [3072, 768], P('head'), may hold values from -0.109375 to 0.109375
- b_down: float32 [768], replicated, may hold values from -2 to 2
Outputs:
- output: bfloat16 [16384, 768], P(('dp', 'head'))
- grad_tokens: float32 [16384, 768], P(('dp', 'head'))
- grad_gain_one: float32 [768], replicated
- grad_shift_one: float32 [768], replicated
- grad_w_query: float32 [768, 768], P(None, 'head')
- grad_b_query: float32 [768], P('head')
- grad_w_key: float32 [768, 768], P(None, 'head')
- grad_w_value: float32 [768, 768], P(None, 'head')
- grad_b_value: float32 [768], P('head')
- grad_w_out: float32 [768, 768], P('head')
- grad_b_out: float32 [768], replicated
- grad_gain_two: float32 [768], replicated
- grad_shift_two: float32 [768], replicated
- grad_w_up: float32 [768, 3072], P(None, 'head')
- grad_b_up: float32 [3072], replicated
- grad_w_down: float32 [3072, 768], P('head')
- grad_b_down: float32 [768], replicated
The draws below stay inside these ranges and needn't reach their ends.
Inputs may be any that keep to these rules, and one draw needn't show every extreme that they name: `segments`: within each aligned run of 512 rows the numbers start at 0, never fall, and rise by one at each of 2 places. `padding`: in each aligned run of 512 rows, the last 1 to 64 rows are 1 and the others 0.
All inputs are finite; a program needn't handle non-finite values.
Results may differ from the reference program's by a relative error of at most 0.014.
The reference program's roundings to bfloat16 on the way count: a program that leaves them out, or rounds other values in their place, can miss the bound.
Values may be sent and summed in bfloat16 or wider, within the bound.
No kernel may reach another device: no remote copies, remote signals or barrier semaphores. Data moves between devices by JAX's collectives and lax.ppermute only.
A program may use at most 192 MiB of HBM per device.

```python
import math
import jax
import jax.numpy as jnp
from jax import lax

D = 768
HEADS = 12
HD = 64
FF = 3072
SEQ = 512
DOCS = 3
TOKENS = 16384


def draw_segments(key, part):
    key = jax.random.fold_in(key, 11)
    seq_count = TOKENS // SEQ
    sub_keys = jax.random.split(key, seq_count)

    def draw_single(sub_key):
        cut_points = jax.random.permutation(sub_key, SEQ - 1)[:DOCS - 1] + 1
        positions = jnp.arange(SEQ, dtype=jnp.int32)
        return jnp.sum((positions[:, None] >= cut_points[None, :]).astype(jnp.int32), axis=1)
    return jax.vmap(draw_single)(sub_keys).reshape(TOKENS).astype(jnp.int32)


def draw_padding(key, part):
    key = jax.random.fold_in(key, 23)
    seq_count = TOKENS // SEQ
    tail_rows = jax.random.randint(key, (seq_count, 1), 1, SEQ // 8 + 1)
    positions = jnp.arange(SEQ, dtype=jnp.int32)[None, :]
    return (positions >= SEQ - tail_rows).astype(jnp.int32).reshape(TOKENS)


def block_scale(key, shape, cuts, smallest, top_value):
    level, own = 1.0, jax.random.fold_in(key, 6)
    for axis_at, shards_of in cuts:
        steps = jnp.exp(jax.random.uniform(jax.random.fold_in(own, axis_at), (shards_of,), jnp.float32, smallest / len(cuts), top_value / len(cuts)))
        level = level * jnp.repeat(steps, shape[axis_at] // shards_of).reshape([-1 if axis == axis_at else 1 for axis in range(len(shape))])
    return level


def bell_draw(stream_key, shape, scale, most, cuts=(), kind=jnp.bfloat16):
    result = scale * jax.random.normal(stream_key, shape, jnp.float32)
    if cuts:
        result = result * block_scale(stream_key, shape, cuts, -0.22, 0.18)
    return jnp.clip(result, -most, most).astype(kind)


def setup_inputs(seed: int = 0) -> dict:
    splits = jax.random.split(jax.random.key(seed), 20)
    return {
        "tokens": bell_draw(splits[0], (TOKENS, D), 1.0, 6.0, ((0, 32),)),
        "segments": draw_segments(jax.random.fold_in(splits[19], 71), 0),
        "padding": draw_padding(jax.random.fold_in(splits[19], 71), 0),
        "cotangent": bell_draw(splits[3], (TOKENS, D), 1.0, 6.0, ((0, 32),)),
        "gain_one": jnp.clip(1.0 + 0.1 * jax.random.normal(splits[4], (D,), jnp.float32), 0.5, 1.5),
        "shift_one": bell_draw(splits[5], (D,), 0.3, 2.0, (), jnp.float32),
        "w_query": bell_draw(splits[6], (D, D), (D // 2) ** -0.5, 0.3125, ((1, 2),)),
        "b_query": bell_draw(splits[7], (D,), 0.5, 3.0, ((0, 2),), jnp.float32),
        "w_key": bell_draw(splits[8], (D, D), (D // 2) ** -0.5, 0.3125, ((1, 2),)),
        "w_value": bell_draw(splits[9], (D, D), D ** -0.5, 0.21875, ((1, 2),)),
        "b_value": bell_draw(splits[10], (D,), 0.5, 3.0, ((0, 2),), jnp.float32),
        "w_out": bell_draw(splits[11], (D, D), (D // 8) ** -0.5, 0.625, ((0, 2),)),
        "b_out": bell_draw(splits[12], (D,), 0.3, 2.0, (), jnp.float32),
        "gain_two": jnp.clip(1.0 + 0.1 * jax.random.normal(splits[13], (D,), jnp.float32), 0.5, 1.5),
        "shift_two": bell_draw(splits[14], (D,), 0.3, 2.0, (), jnp.float32),
        "w_up": bell_draw(splits[15], (D, FF), D ** -0.5, 0.21875, ((1, 2),)),
        "b_up": bell_draw(splits[16], (FF,), 0.3, 2.0, (), jnp.float32),
        "w_down": bell_draw(splits[17], (FF, D), FF ** -0.5, 0.109375, ((0, 2),)),
        "b_down": bell_draw(splits[18], (D,), 0.3, 2.0, (), jnp.float32),
    }


epsilon = 1e-06
highest = lax.Precision.HIGHEST

@jax.custom_vjp
def low(v):
    return lax.optimization_barrier(v.astype(jnp.bfloat16)).astype(jnp.float32)

@jax.custom_vjp
def low_back(v):
    return v

def low_keep(v):
    return (low(v), None)

def low_pass(kept, grad):
    return (grad,)

def back_keep(v):
    return (v, None)

def back_low(kept, grad):
    return (low(grad),)
low.defvjp(low_keep, low_pass)
low_back.defvjp(back_keep, back_low)

def layer_norm(row_block, norm_gain, norm_shift):
    centre = lax.optimization_barrier(jnp.mean(row_block, axis=-1, keepdims=True))
    shifted = row_block - centre
    spread = lax.optimization_barrier(jnp.mean(shifted * shifted, axis=-1, keepdims=True))
    return shifted * lax.rsqrt(spread + epsilon) * norm_gain + norm_shift

def product(left_side, right_side):
    return jnp.dot(left_side, right_side, precision=highest, preferred_element_type=jnp.float32)

def attend_one(inputs):
    queries, keys_seq, values_seq, segment, padding = inputs
    length = segment.shape[0]
    score_scale = queries.shape[-1] ** (-0.5)
    scores = jnp.einsum('qhd,khd->hqk', queries, keys_seq, precision=highest, preferred_element_type=jnp.float32)
    scores = low_back(scores * score_scale)
    positions = jnp.arange(length)
    allowed = (segment[:, None] == segment[None, :]) & ((padding[None, :] == 0) | (positions[:, None] == positions[None, :]))
    masked = jnp.where(allowed[None], scores, -1e+30)
    probabilities = low(jax.nn.softmax(masked, axis=-1))
    return jnp.einsum('hqk,khd->qhd', probabilities, values_seq, precision=highest, preferred_element_type=jnp.float32)

def forward(params, row_block, segment, padding):
    gain_one, shift_one, w_query, b_query, w_key, w_value, b_value, w_out, b_out, gain_two, shift_two, w_up, b_up, w_down, b_down = params
    normed = low(layer_norm(row_block, gain_one, shift_one))
    queries = low(low_back(product(normed, w_query) + b_query))
    keys_all = low(low_back(product(normed, w_key)))
    values_all = low(low_back(product(normed, w_value) + b_value))
    seq_count = row_block.shape[0] // SEQ

    def per_sequence(block_rows):
        return block_rows.reshape(seq_count, SEQ, HEADS, HD)
    mixed = lax.map(jax.checkpoint(attend_one), (per_sequence(queries), per_sequence(keys_all), per_sequence(values_all), segment.reshape(seq_count, SEQ), padding.reshape(seq_count, SEQ)))
    context = low(low_back(mixed.reshape(row_block.shape[0], D)))
    hidden = row_block + low_back(product(context, w_out) + b_out)
    normed_two = low(layer_norm(hidden, gain_two, shift_two))
    gate = low_back(product(normed_two, w_up) + b_up)
    active = low(jax.nn.gelu(gate, approximate=False))
    return hidden + low_back(product(active, w_down) + b_down)

def reference(tokens, segments, padding, cotangent, gain_one, shift_one, w_query, b_query, w_key, w_value, b_value, w_out, b_out, gain_two, shift_two, w_up, b_up, w_down, b_down):
    params = tuple((weight.astype(jnp.float32) for weight in (gain_one, shift_one, w_query, b_query, w_key, w_value, b_value, w_out, b_out, gain_two, shift_two, w_up, b_up, w_down, b_down)))
    total_rows = tokens.shape[0]
    group_rows = math.gcd(total_rows // SEQ, 8) * SEQ
    group_count = total_rows // group_rows

    def scan_step(totals, pieces):
        row_block, seg_block, pad_block, grad_block = pieces
        outcome, pullback = jax.vjp(lambda weights, inputs: forward(weights, inputs, seg_block, pad_block), params, row_block)
        keep_rows = (1 - pad_block).astype(jnp.float32)[:, None]
        grad_weights, grad_rows = pullback(grad_block * keep_rows)
        totals = jax.tree.map(jnp.add, totals, grad_weights)
        return (totals, (outcome.astype(jnp.bfloat16), grad_rows))
    zeros_tree = jax.tree.map(jnp.zeros_like, params)
    stacked = (tokens.astype(jnp.float32).reshape(group_count, group_rows, D), segments.reshape(group_count, group_rows), padding.reshape(group_count, group_rows), cotangent.astype(jnp.float32).reshape(group_count, group_rows, D))
    totals, (outputs, grad_rows) = lax.scan(scan_step, zeros_tree, stacked)
    return (outputs.reshape(total_rows, D), grad_rows.reshape(total_rows, D), totals[0], totals[1], totals[2], totals[3], totals[4], totals[5], totals[6], totals[7], totals[8], totals[9], totals[10], totals[11], totals[12], totals[13], totals[14])
```

```python
import jax
import jax.numpy as jnp
from jax import lax
from jax.sharding import PartitionSpec as P

HD = 64
SEQ = 512
epsilon = 1e-06
BF = jnp.bfloat16
F32 = jnp.float32


def layer_norm(row_block, norm_gain, norm_shift):
    centre = jnp.mean(row_block, axis=-1, keepdims=True)
    shifted = row_block - centre
    spread = jnp.mean(shifted * shifted, axis=-1, keepdims=True)
    return shifted * lax.rsqrt(spread + epsilon) * norm_gain + norm_shift


def exact_gelu(values_in):
    return jax.nn.gelu(values_in, approximate=False)


def matmul(left_side, right_side):
    return jnp.dot(left_side, right_side, preferred_element_type=F32)


def inner_product(left_side, right_side):
    return lax.dot_general(
        left_side, right_side, (((0,), (0,)), ((), ())), preferred_element_type=F32
    )


def across(left_side, right_side):
    return lax.dot_general(
        left_side, right_side, (((1,), (1,)), ((), ())), preferred_element_type=F32
    )


def column_sums(matrix):
    return jnp.sum(matrix.astype(F32), axis=0)


def attend_forward(queries, keys, values, bias):
    heads = queries.shape[1] // HD
    q = queries.reshape(SEQ, heads, HD)
    k = keys.reshape(SEQ, heads, HD)
    v = values.reshape(SEQ, heads, HD)
    scores = jnp.einsum("qhd,khd->hqk", q, k, preferred_element_type=F32) * (HD**-0.5)
    masked = jnp.where(bias[None], scores, -1e30)
    top = jnp.max(masked, axis=-1, keepdims=True)
    raised = jnp.exp(masked - top)
    total = jnp.sum(raised, axis=-1, keepdims=True)
    low = (raised / total).astype(BF)
    context = jnp.einsum("hqk,khd->qhd", low, v, preferred_element_type=F32)
    return context.reshape(SEQ, -1).astype(BF), top + jnp.log(total)


def attend_backward(queries, keys, values, bias, lse, grad_context):
    heads = queries.shape[1] // HD
    q = queries.reshape(SEQ, heads, HD)
    k = keys.reshape(SEQ, heads, HD)
    v = values.reshape(SEQ, heads, HD)
    g = grad_context.reshape(SEQ, heads, HD)
    scale = HD**-0.5
    scores = jnp.einsum("qhd,khd->hqk", q, k, preferred_element_type=F32) * scale
    probs = jnp.exp(jnp.where(bias[None], scores, -1e30) - lse)
    low = probs.astype(BF)
    grad_v = jnp.einsum("hqk,qhd->khd", low, g, preferred_element_type=F32)
    grad_p = jnp.einsum("qhd,khd->hqk", g, v, preferred_element_type=F32)
    grad_s = probs * (grad_p - jnp.sum(grad_p * probs, axis=-1, keepdims=True))
    grad_s = grad_s.astype(BF)
    grad_q = jnp.einsum("hqk,khd->qhd", grad_s, k, preferred_element_type=F32) * scale
    grad_k = jnp.einsum("hqk,qhd->khd", grad_s, q, preferred_element_type=F32) * scale
    return tuple(t.reshape(SEQ, -1).astype(BF) for t in (grad_q, grad_k, grad_v))


def make_per_device(dp_size):
    bits = dp_size.bit_length() - 1
    assert dp_size == 1 << bits

    def swap(value, level):
        if level == "h":
            return lax.ppermute(value, "head", [(0, 1), (1, 0)])
        return lax.ppermute(value, "dp", [(i, i ^ (1 << level)) for i in range(dp_size)])

    def my_bit(level):
        return (lax.axis_index("dp") >> level) & 1

    def pick(value, axis, index):
        return lax.dynamic_index_in_dim(value, index, axis, keepdims=False)

    def split(value):
        rows = value.shape[0]
        return value.reshape((2,) * bits + (rows >> bits,) + value.shape[1:])

    def reduce_scatter(own, other, order):
        own, other = split(own), split(other)
        left = list(range(bits))
        for level in order:
            if level == "h":
                own = (own.astype(F32) + swap(other, "h").astype(F32)).astype(BF)
                other = None
                continue
            axis = left.index(level)
            left.remove(level)
            b = my_bit(level)

            def exchange(v):
                got = swap(pick(v, axis, 1 - b), level)
                return (pick(v, axis, b).astype(F32) + got.astype(F32)).astype(BF)

            own = exchange(own)
            if other is not None:
                other = exchange(other)
        return own

    def all_gather(piece, order):
        left = []
        for level in order:
            axis = sum(1 for q in left if q < level)
            left.append(level)
            got = swap(piece, level)
            b = my_bit(level)
            shape = piece.shape[:axis] + (2,) + piece.shape[axis:]
            full = jnp.zeros(shape, piece.dtype)
            full = lax.dynamic_update_index_in_dim(full, piece, b, axis)
            piece = lax.dynamic_update_index_in_dim(full, got, 1 - b, axis)
        rows = piece.shape[bits]
        return piece.reshape((rows << bits,) + piece.shape[bits + 1 :])

    def fetch_other(weight):
        quarters = weight.reshape((2, 2, weight.shape[0] // 4) + weight.shape[1:])
        c, x = my_bit(0), my_bit(1)
        first = swap(pick(pick(quarters, 0, c), 0, x), "h")
        second = swap(first, 1)
        both = jnp.zeros((2,) + first.shape, first.dtype)
        both = lax.dynamic_update_index_in_dim(both, first, x, 0)
        both = lax.dynamic_update_index_in_dim(both, second, 1 - x, 0)
        rest = swap(both, 0)
        full = jnp.zeros((2,) + both.shape, both.dtype)
        full = lax.dynamic_update_index_in_dim(full, both, c, 0)
        full = lax.dynamic_update_index_in_dim(full, rest, 1 - c, 0)
        return full.reshape(weight.shape)

    def per_device(
        tokens, segments, padding, cotangent, gain_one, shift_one, w_query, b_query, w_key,
        w_value, b_value, w_out, b_out, gain_two, shift_two, w_up, b_up, w_down, b_down,
    ):
        rows = tokens.shape[0]
        assert rows == SEQ
        y = lax.axis_index("head")
        own_pad = lax.dynamic_slice_in_dim(padding, y * rows, rows)
        own_seg = lax.dynamic_slice_in_dim(segments, y * rows, rows)
        half = w_query.shape[1]
        hid = w_up.shape[1]

        qkv_own = jnp.concatenate((w_query, w_key, w_value), axis=1)
        qkv_oth = fetch_other(qkv_own)
        bias_own = jnp.stack((b_query, b_value))
        bias_oth = swap(bias_own, "h")
        out_oth = fetch_other(w_out)
        up_oth = fetch_other(w_up)
        down_oth = fetch_other(w_down)

        start_rows = tokens.astype(F32)
        normed, first_pull = jax.vjp(layer_norm, start_rows, gain_one, shift_one)
        normed = normed.astype(BF)
        positions = jnp.arange(rows)
        allowed = (own_seg[:, None] == own_seg[None, :]) & (
            (own_pad[None, :] == 0) | (positions[:, None] == positions[None, :])
        )

        def project(w, b):
            z = matmul(normed, w)
            return (
                (z[:, :half] + b[0]).astype(BF),
                z[:, half : 2 * half].astype(BF),
                (z[:, 2 * half :] + b[1]).astype(BF),
            )

        qkv1 = project(qkv_own, bias_own)
        ctx1, lse1 = attend_forward(*qkv1, allowed)
        qkv2 = project(qkv_oth, bias_oth)
        ctx2, lse2 = attend_forward(*qkv2, allowed)
        hidden = start_rows + (matmul(ctx1, w_out) + matmul(ctx2, out_oth)) + b_out
        normed_two, second_pull = jax.vjp(layer_norm, hidden, gain_two, shift_two)
        up_in = normed_two.astype(BF)
        grad_out = cotangent.astype(F32) * (1 - own_pad).astype(F32)[:, None]
        down_grad = grad_out.astype(BF)

        def feed(w_u, b_u, w_d):
            gate = matmul(up_in, w_u) + b_u
            active, gelu_pull = jax.vjp(exact_gelu, gate)
            active = active.astype(BF)
            (grad_gate,) = gelu_pull(across(down_grad, w_d))
            grad_gate = grad_gate.astype(BF)
            return (
                matmul(active, w_d),
                across(grad_gate, w_u),
                inner_product(up_in, grad_gate).astype(BF),
                inner_product(active, down_grad).astype(BF),
                column_sums(grad_gate),
            )

        bu_own = lax.dynamic_slice_in_dim(b_up, y * hid, hid)
        bu_oth = lax.dynamic_slice_in_dim(b_up, (1 - y) * hid, hid)
        o1, u1, gu1, gd1, gb1 = feed(w_up, bu_own, w_down)
        o2, u2, gu2, gd2, gb2 = feed(up_oth, bu_oth, down_oth)
        order_y = (0, "h") + tuple(range(1, bits))
        order_x = (0, 1, "h") + tuple(range(2, bits))
        gather = tuple(range(bits - 1, -1, -1))

        def finish(own, other, order):
            return all_gather(reduce_scatter(own, other, order), gather)

        grad_w_up = finish(gu1, gu2, order_y).astype(F32)
        grad_w_down = finish(gd1, gd2, order_x).astype(F32)
        output = (hidden + (o1 + o2) + b_down).astype(BF)
        grad_hidden_norm, grad_gain_two, grad_shift_two = second_pull(u1 + u2)
        grad_hidden = grad_out + grad_hidden_norm
        attn_grad = grad_hidden.astype(BF)
        gc1 = across(attn_grad, w_out).astype(BF)
        gc2 = across(attn_grad, out_oth).astype(BF)
        go1 = inner_product(ctx1, attn_grad).astype(BF)
        go2 = inner_product(ctx2, attn_grad).astype(BF)
        grad_w_out = finish(go1, go2, order_y).astype(F32)

        def attention_back(qkv, lse, gc, w):
            grads = jnp.concatenate(attend_backward(*qkv, allowed, lse, gc), axis=1)
            return grads, inner_product(normed, grads).astype(BF), across(grads, w)

        gs2, gw2, gn2 = attention_back(qkv2, lse2, gc2, qkv_oth)
        gs1, gw1, gn1 = attention_back(qkv1, lse1, gc1, qkv_own)
        grad_qkv = finish(gw1, gw2, order_y).astype(F32)
        grad_rows, grad_gain_one, grad_shift_one = first_pull(gn1 + gn2)
        grad_tokens = grad_hidden + grad_rows

        def absolute(own, oth):
            return jnp.where(y == 0, jnp.concatenate((own, oth)), jnp.concatenate((oth, own)))

        sb1, sb2 = column_sums(gs1), column_sums(gs2)
        small = [
            grad_gain_one,
            grad_shift_one,
            column_sums(attn_grad),
            grad_gain_two,
            grad_shift_two,
            column_sums(down_grad),
            absolute(gb1, gb2),
            absolute(sb1[:half], sb2[:half]),
            absolute(sb1[2 * half :], sb2[2 * half :]),
        ]
        packed = lax.psum(jnp.concatenate(small), ("dp", "head"))
        parts, at = [], 0
        for s in small:
            parts.append(packed[at : at + s.shape[0]])
            at += s.shape[0]
        gg1, gs_1, gbo, gg2, gs_2, gbd, gbu, gbq, gbv = parts
        return (
            output,
            grad_tokens,
            gg1,
            gs_1,
            grad_qkv[:, :half],
            lax.dynamic_slice_in_dim(gbq, y * half, half),
            grad_qkv[:, half : 2 * half],
            grad_qkv[:, 2 * half :],
            lax.dynamic_slice_in_dim(gbv, y * half, half),
            grad_w_out,
            gbo,
            gg2,
            gs_2,
            grad_w_up,
            gbu,
            grad_w_down,
            gbd,
        )

    return per_device


def solution(mesh):
    rows, heads = P(("dp", "head"), None), P("head")
    columns, lines = P(None, "head"), P("head", None)
    in_specs = (
        rows, P("dp"), P("dp"), rows, P(), P(), columns, heads, columns, columns, heads,
        lines, P(), P(), P(), columns, P(), lines, P(),
    )
    out_specs = (
        rows, rows, P(), P(), columns, heads, columns, columns, heads, lines, P(), P(), P(),
        columns, P(), lines, P(),
    )
    return jax.shard_map(
        make_per_device(mesh.shape["dp"]),
        mesh=mesh,
        in_specs=in_specs,
        out_specs=out_specs,
        check_vma=False,
    )
```

```python
import functools

import jax
import jax.numpy as jnp
from jax import lax
from jax.experimental import pallas as pl
from jax.experimental.pallas import tpu as pltpu
from jax.sharding import PartitionSpec as P

HD = 64
SEQ = 512
PAIR = 2 * HD
BLOCK = 256
epsilon = 1e-06
BF = jnp.bfloat16
F32 = jnp.float32
VMEM_LIMIT = 56 * 1024 * 1024


def mm(a, b):
    return lax.dot_general(a, b, (((1,), (0,)), ((), ())), preferred_element_type=F32)


def nt(a, b):
    return lax.dot_general(a, b, (((1,), (1,)), ((), ())), preferred_element_type=F32)


def tn(a, b):
    return lax.dot_general(a, b, (((0,), (0,)), ((), ())), preferred_element_type=F32)


def full(shape):
    return pl.BlockSpec(shape, lambda *_: (0,) * len(shape))


def call(
    kernel, outs, args, flops=0, grid=None, in_specs=None, out_specs=None, scratch=(), prefetch=0
):
    spec = pltpu.PrefetchScalarGridSpec(
        num_scalar_prefetch=prefetch,
        grid=grid or (1,),
        in_specs=in_specs or [full(a.shape) for a in args[prefetch:]],
        out_specs=out_specs or [full(s) for s, _ in outs],
        scratch_shapes=scratch,
    )
    moved = sum(a.size * a.dtype.itemsize for a in args)
    return pl.pallas_call(
        kernel,
        grid_spec=spec,
        out_shape=[jax.ShapeDtypeStruct(s, t) for s, t in outs],
        compiler_params=pltpu.CompilerParams(vmem_limit_bytes=VMEM_LIMIT),
        cost_estimate=pl.CostEstimate(
            flops=int(flops), bytes_accessed=int(moved), transcendentals=0
        ),
    )(*args)


def norm_parts(v):
    centre = jnp.mean(v, axis=-1, keepdims=True)
    shifted = v - centre
    spread = jnp.mean(shifted * shifted, axis=-1, keepdims=True)
    r = lax.rsqrt(spread + epsilon)
    return shifted * r, r


def norm_back(e, xhat, r, gain):
    eg = e * gain
    mean_eg = jnp.mean(eg, axis=-1, keepdims=True)
    return r * (eg - mean_eg - xhat * jnp.mean(eg * xhat, axis=-1, keepdims=True))


def column(row):
    return jnp.transpose(jnp.broadcast_to(row, (128, row.shape[1])))[:, :1]


def fill_bias(seg_ref, pad_ref, bias_ref):
    seg = seg_ref[...].astype(F32)
    seg_col, pad_col = column(seg), column(pad_ref[...].astype(F32))
    for b in range(SEQ // BLOCK):
        cols = slice(b * BLOCK, (b + 1) * BLOCK)
        key = lax.broadcasted_iota(jnp.int32, (SEQ, BLOCK), 0)
        query = lax.broadcasted_iota(jnp.int32, (SEQ, BLOCK), 1) + b * BLOCK
        ok = (seg_col == seg[:, cols]) & ((pad_col == 0) | (key == query))
        bias_ref[:, cols] = jnp.where(ok, 0.0, -1e30)


def attend_pair(q2, k2, v2, bias_ref, lse_ref, at):
    lane = lax.broadcasted_iota(jnp.int32, (SEQ, PAIR), 1)
    row = lax.broadcasted_iota(jnp.int32, (PAIR, SEQ), 0)
    q2 = q2 * BF(HD**-0.5)
    vt = jnp.transpose(v2)
    found = []
    for b in range(SEQ // BLOCK):
        rows = slice(b * BLOCK, (b + 1) * BLOCK)
        total = None
        for e in range(2):
            qe = jnp.where((lane[rows] // HD) == e, q2[rows], BF(0))
            s = nt(k2, qe) + bias_ref[:, rows]
            top = jnp.max(s, axis=0, keepdims=True)
            raised = jnp.exp(s - top)
            den = jnp.sum(raised, axis=0, keepdims=True)
            low = (raised * (1.0 / den)).astype(BF)
            ve = jnp.where((row // HD) == e, vt, BF(0))
            part = mm(ve, low)
            total = part if total is None else total + part
            lse_ref[at + e : at + e + 1, rows] = top + jnp.log(den)
        found.append(jnp.transpose(total).astype(BF))
    return jnp.concatenate(found, axis=0)


def first_kernel(
    half, tok, cot, seg, pad, g1, s1, wq, wk, wv, bq, bv, n1_ref, dn_ref, qkv_ref, ctx_ref, lse_ref, bias_ref,
):
    xhat, _ = norm_parts(tok[...].astype(F32))
    n1 = (xhat * g1[...] + s1[...]).astype(BF)
    n1_ref[...] = n1
    keep = column(1.0 - pad[...].astype(F32))
    dn_ref[...] = (cot[...].astype(F32) * keep).astype(BF)
    fill_bias(seg, pad, bias_ref)
    qkv_ref[:, :half] = (mm(n1, wq[...]) + bq[...]).astype(BF)
    qkv_ref[:, half : 2 * half] = mm(n1, wk[...]).astype(BF)
    qkv_ref[:, 2 * half :] = (mm(n1, wv[...]) + bv[...]).astype(BF)
    for p in range(half // PAIR):
        q2, k2, v2 = (
            qkv_ref[:, m * half + p * PAIR : m * half + (p + 1) * PAIR] for m in range(3)
        )
        ctx_ref[:, p * PAIR : (p + 1) * PAIR] = attend_pair(q2, k2, v2, bias_ref, lse_ref, 2 * p)


def pair_kernel(c_ref, n1, seg, pad, w_mine, w_rest, bias3, qkv_ref, ctx_ref, lse_ref, w_ref, bias_ref):
    d2 = w_mine.shape[0]
    c = c_ref[0]
    fill_bias(seg, pad, bias_ref)
    w_ref[pl.ds(c * d2, d2), :] = w_mine[...]
    w_ref[pl.ds((1 - c) * d2, d2), :] = w_rest[...]
    z = (mm(n1[...], w_ref[...]) + bias3[...]).astype(BF)
    qkv_ref[...] = z
    ctx_ref[...] = attend_pair(
        z[:, :PAIR], z[:, PAIR : 2 * PAIR], z[:, 2 * PAIR :], bias_ref, lse_ref, 0
    )


def hidden_kernel(pairs, c_ref, tok, ctx1, *rest):
    ctx_refs = rest[:pairs]
    wo1, wo_mine, wo_rest, bo, g2, s2, ctx2_ref, wo2_ref, hid_ref, n2_ref = rest[pairs:]
    c = c_ref[0]
    r2 = wo_mine.shape[0]
    wo2_ref[pl.ds(c * r2, r2), :] = wo_mine[...]
    wo2_ref[pl.ds((1 - c) * r2, r2), :] = wo_rest[...]
    for p in range(pairs):
        ctx2_ref[:, p * PAIR : (p + 1) * PAIR] = ctx_refs[p][...]
    mixed = mm(ctx1[...], wo1[...]) + mm(ctx2_ref[...], wo2_ref[...])
    hidden = tok[...].astype(F32) + mixed + bo[...]
    hid_ref[...] = hidden
    xhat, _ = norm_parts(hidden)
    n2_ref[...] = (xhat * g2[...] + s2[...]).astype(BF)


def feed_step(n2, dn, wu, bu, wd):
    gate = mm(n2, wu) + bu
    dact = nt(dn, wd)
    cdf = 0.5 * (1.0 + lax.erf(gate * (0.5**0.5)))
    pdf = jnp.exp(gate * gate * -0.5) * 0.3989422804014327
    act = (gate * cdf).astype(BF)
    gg = (dact * (cdf + gate * pdf)).astype(BF)
    return act, gg


def feed_kernel(fetched, at_ref, n2, dn, bu, *rest):
    j = pl.program_id(0)
    if fetched:
        parts, rest = rest[:8], rest[8:]
        out_in, upb_in, *rest = rest
        wu, wd = rest[-2:]
        for k in range(4):

            @pl.when(j == k)
            def _(k=k):
                wu[...] = parts[k][...]
                wd[...] = parts[4 + k][...]
    else:
        wu, wd, *rest = rest
    out_ref, upb_ref, gu_s, gu_k, gd_s, gd_k, gb_ref = rest[:7]
    act, gg = feed_step(n2[...], dn[...], wu[...], bu[...], wd[...])

    @pl.when(j == 0)
    def _():
        out_ref[...] = (out_in[...] if fetched else 0.0) + mm(act, wd[...])
        upb_ref[...] = (upb_in[...] if fetched else 0.0) + nt(gg, wu[...])

    @pl.when(j > 0)
    def _():
        out_ref[...] += mm(act, wd[...])
        upb_ref[...] += nt(gg, wu[...])

    gb_ref[...] = jnp.sum(gg.astype(F32), axis=0, keepdims=True)
    gu = tn(n2[...], gg).astype(BF)
    gd = tn(act, dn[...]).astype(BF)

    @pl.when(j < 2)
    def _():
        gu_s[...] = gu
        gd_s[...] = gd

    @pl.when(j >= 2)
    def _():
        gu_k[...] = gu
        gd_k[...] = gd


def feed(where, n2, dn, bu, weights, before=None):
    d = n2.shape[1]
    hid = bu.shape[1]
    step = hid // 4

    def side(j, at):
        return at[1] ^ (j % 2)

    def block(j, at):
        return jnp.where(j < 2, 1 - at[0], at[0]) * 2 + side(j, at)

    def sent(j, at):
        return at[1] ^ jnp.minimum(j, 1)

    def kept(j, at):
        return at[1] ^ jnp.maximum(j - 2, 0)

    const = pl.BlockSpec((SEQ, d), lambda j, at: (0, 0))
    fetched = before is not None
    if fetched:
        weight_specs = [full(w.shape) for w in weights] + [const, const]
        scratch = [pltpu.VMEM((d, step), BF), pltpu.VMEM((step, d), BF)]
    else:
        weight_specs = [
            pl.BlockSpec((d, step), lambda j, at: (0, block(j, at))),
            pl.BlockSpec((step, d), lambda j, at: (block(j, at), 0)),
        ]
        scratch = []
    args = [where, n2, dn, bu] + list(weights) + list(before or ())
    return call(
        functools.partial(feed_kernel, fetched),
        [((SEQ, d), F32)] * 2
        + [((d, hid // 2), BF)] * 2
        + [((hid // 2, d), BF)] * 2
        + [((1, hid), F32)],
        args,
        flops=16e9,
        grid=(4,),
        in_specs=[const, const, pl.BlockSpec((1, step), lambda j, at: (0, block(j, at)))]
        + weight_specs,
        out_specs=[
            const,
            const,
            pl.BlockSpec((d, step), lambda j, at: (0, sent(j, at))),
            pl.BlockSpec((d, step), lambda j, at: (0, kept(j, at))),
            pl.BlockSpec((step, d), lambda j, at: (sent(j, at), 0)),
            pl.BlockSpec((step, d), lambda j, at: (kept(j, at), 0)),
            pl.BlockSpec((1, step), lambda j, at: (0, block(j, at))),
        ],
        scratch=scratch,
        prefetch=1,
    )


def middle_kernel(
    hid, out_acc, upb, dn, bd, g2, ctx1, ctx2, wo1, wo2, out_ref, gh_ref, small_ref, gc1_ref, gc2_ref, go1_ref, go2_ref,
):
    hidden = hid[...]
    out_ref[...] = (hidden + out_acc[...] + bd[...]).astype(BF)
    xhat, r = norm_parts(hidden)
    e = upb[...]
    dn_f = dn[...].astype(F32)
    grad_hidden = dn_f + norm_back(e, xhat, r, g2[...])
    gh_ref[...] = grad_hidden
    ag = grad_hidden.astype(BF)
    small_ref[0:1] = jnp.sum(e * xhat, axis=0, keepdims=True)
    small_ref[1:2] = jnp.sum(e, axis=0, keepdims=True)
    small_ref[2:3] = jnp.sum(ag.astype(F32), axis=0, keepdims=True)
    small_ref[3:4] = jnp.sum(dn_f, axis=0, keepdims=True)
    gc1_ref[...] = nt(ag, wo1[...]).astype(BF)
    gc2_ref[...] = nt(ag, wo2[...]).astype(BF)
    go1_ref[...] = tn(ctx1[...], ag).astype(BF)
    go2_ref[...] = tn(ctx2[...], ag).astype(BF)


def attend_pair_back(q2, k2, v2, g2, bias_ref, lse_ref, at):
    lane = lax.broadcasted_iota(jnp.int32, (SEQ, PAIR), 1)
    row = lax.broadcasted_iota(jnp.int32, (PAIR, SEQ), 0)
    q2 = q2 * BF(HD**-0.5)
    kt = jnp.transpose(k2)
    dq, dk, dv = [], None, None
    for b in range(SEQ // BLOCK):
        rows = slice(b * BLOCK, (b + 1) * BLOCK)
        dqt = None
        for e in range(2):
            on = (lane[rows] // HD) == e
            qe = jnp.where(on, q2[rows], BF(0))
            ge = jnp.where(on, g2[rows], BF(0))
            ke = jnp.where((row // HD) == e, kt, BF(0))
            s = nt(k2, qe) + bias_ref[:, rows]
            probs = jnp.exp(s - lse_ref[at + e : at + e + 1, rows])
            gp = nt(v2, ge)
            delta = jnp.sum(gp * probs, axis=0, keepdims=True)
            gs = (probs * (gp - delta)).astype(BF)
            t = mm(probs.astype(BF), ge)
            dv = t if dv is None else dv + t
            t = mm(gs, qe)
            dk = t if dk is None else dk + t
            t = mm(ke, gs)
            dqt = t if dqt is None else dqt + t
        dq.append((jnp.transpose(dqt) * (HD**-0.5)).astype(BF))
    return jnp.concatenate(dq, axis=0), dk.astype(BF), dv.astype(BF)


def pack_out(dst_ref, at, piece):
    r, n = piece.shape
    tall = jnp.concatenate((piece[:, : n // 2], piece[:, n // 2 :]), axis=0)
    cut = 2 * r // 3
    for k in range(3):
        dst_ref[at : at + cut, k * (n // 2) : (k + 1) * (n // 2)] = tall[k * cut : (k + 1) * cut]


def qkv_back_kernel(half, own, c_ref, n1, gc, go, seg, pad, *rest):
    pairs = half // PAIR
    if own:
        qkv, lse, wq, wk, wv, dn1_in, tok, gh, g1, *rest = rest
        gws_ref, gwk_ref, sums_ref, gt_ref, small_ref, bias_ref, grad_ref = rest
    else:
        qkvs, lses, ws = rest[:pairs], rest[pairs : 2 * pairs], rest[2 * pairs : 3 * pairs]
        gws_ref, gwk_ref, sums_ref, dn1_ref, bias_ref, grad_ref, w_ref = rest[3 * pairs :]
    fill_bias(seg, pad, bias_ref)
    for p in range(pairs):
        at = [slice(m * half + p * PAIR, m * half + (p + 1) * PAIR) for m in range(3)]
        if own:
            q2, k2, v2 = (qkv[:, at[m]] for m in range(3))
            found = attend_pair_back(q2, k2, v2, gc[:, at[0]], bias_ref, lse, 2 * p)
        else:
            q2, k2, v2 = (qkvs[p][:, m * PAIR : (m + 1) * PAIR] for m in range(3))
            found = attend_pair_back(q2, k2, v2, gc[:, at[0]], bias_ref, lses[p], 0)
            for m in range(3):
                w_ref[:, at[m]] = ws[p][:, m * PAIR : (m + 1) * PAIR]
        for m in range(3):
            grad_ref[:, at[m]] = found[m]
    sums_ref[...] = jnp.sum(grad_ref[...].astype(F32), axis=0, keepdims=True)
    d = n1.shape[1]
    c = c_ref[0]
    gw = tn(n1[...], grad_ref[...]).astype(BF)
    top, low = gw[: d // 2], gw[d // 2 :]
    gws_ref[: d // 2] = jnp.where(c == 0, low, top)
    gwk_ref[: d // 2] = jnp.where(c == 0, top, low)
    top, low = go[: half // 2], go[half // 2 :]
    pack_out(gws_ref, d // 2, jnp.where(c == 0, low, top))
    pack_out(gwk_ref, d // 2, jnp.where(c == 0, top, low))
    if not own:
        dn1_ref[...] = nt(grad_ref[...], w_ref[...])
        return
    e = dn1_in[...]
    for m, w in enumerate((wq, wk, wv)):
        e = e + nt(grad_ref[:, m * half : (m + 1) * half], w[...])
    xhat, r = norm_parts(tok[...].astype(F32))
    gt_ref[...] = gh[...] + norm_back(e, xhat, r, g1[...])
    small_ref[0:1] = jnp.sum(e * xhat, axis=0, keepdims=True)
    small_ref[1:2] = jnp.sum(e, axis=0, keepdims=True)


def make_per_device(dp_size):
    bits = dp_size.bit_length() - 1
    assert dp_size == 1 << bits
    levels = tuple(range(1, bits))

    def swap(value, level):
        if level == "h":
            return lax.ppermute(value, "head", [(0, 1), (1, 0)])
        return lax.ppermute(value, "dp", [(i, i ^ (1 << level)) for i in range(dp_size)])

    def my_bit(level):
        return (lax.axis_index("dp") >> level) & 1

    def pick(value, axis, index):
        return lax.dynamic_index_in_dim(value, index, axis, keepdims=False)

    def plus(a, b):
        return (a.astype(F32) + b.astype(F32)).astype(BF)

    def after(value, *others):
        return lax.optimization_barrier((value,) + others)[0]

    class Sum:
        def __init__(self, own, oth, order):
            n = len(levels)
            cut = lambda v: v.reshape((2,) * n + (v.shape[0] >> n,) + v.shape[1:])
            self.own, self.oth = cut(own), None if oth is None else cut(oth)
            self.left, self.order, self.back = list(levels), list(order), list(levels[::-1])

        def half(self, v, axis, level):
            b = my_bit(level)
            return plus(pick(v, axis, b), swap(pick(v, axis, 1 - b), level))

        def step(self):
            level = self.order.pop(0)
            if level == "h":
                self.own, self.oth = plus(self.own, swap(self.oth, "h")), None
                return
            axis = self.left.index(level)
            self.left.remove(level)
            self.own = self.half(self.own, axis, level)
            if self.oth is not None:
                self.oth = self.half(self.oth, axis, level)

        def widen(self):
            level = self.back.pop(0)
            axis = sum(1 for q in self.left if q < level)
            self.left.append(level)
            got = swap(self.own, level)
            low = my_bit(level) == 0
            pair = (jnp.where(low, self.own, got), jnp.where(low, got, self.own))
            self.own = jnp.stack(pair, axis=axis)

        def run(self, steps):
            for _ in range(steps):
                self.step() if self.order else self.widen()
            return self.own

        def finish(self):
            self.run(len(self.order) + len(self.back))
            n = len(levels)
            part = self.own.reshape((self.own.shape[n] << n,) + self.own.shape[n + 1 :])
            got = swap(part, 0)
            low = my_bit(0) == 0
            return jnp.where(low, part, got), jnp.where(low, got, part)

    def per_device(
        tokens, segments, padding, cotangent, gain_one, shift_one, w_query, b_query, w_key,
        w_value, b_value, w_out, b_out, gain_two, shift_two, w_up, b_up, w_down, b_down,
    ):
        rows, d = tokens.shape
        assert rows == SEQ
        y = lax.axis_index("head")
        c, x = my_bit(0), my_bit(1)
        pad = lax.dynamic_slice_in_dim(padding, y * rows, rows)[None]
        seg = lax.dynamic_slice_in_dim(segments, y * rows, rows)[None]
        half = w_query.shape[1]
        pairs = half // PAIR
        hid = w_up.shape[1]
        core = jnp.reshape(c, (1,)).astype(jnp.int32)
        where = jnp.stack((c, x)).astype(jnp.int32)

        square = pltpu.VMEM((SEQ, SEQ), F32)
        row = lambda v: v[None]
        n1, dn, qkv1, ctx1, lse1 = call(
            functools.partial(first_kernel, half),
            [((SEQ, d), BF)] * 2 + [((SEQ, 3 * half), BF), ((SEQ, half), BF), ((8, SEQ), F32)],
            (tokens, cotangent, seg, pad, row(gain_one), row(shift_one), w_query, w_key, w_value,
             row(b_query), row(b_value)),
            flops=8e9,
            scratch=[square],
        )

        mine, rest = [], []
        for p in range(pairs):
            piece = jnp.concatenate(
                [
                    lax.dynamic_slice(w, (c * (d // 2), p * PAIR), (d // 2, PAIR))
                    for w in (w_query, w_key, w_value)
                ],
                axis=1,
            )
            mine.append(swap(piece, "h"))
            rest.append(swap(after(mine[-1], n1), 0))
        bias_oth = swap(jnp.stack((b_query, b_value)), "h")
        out_piece = lax.dynamic_slice_in_dim(w_out, c * (half // 2), half // 2)
        out_mine = swap(after(out_piece, mine[0]), "h")
        out_rest = swap(out_mine, 0)
        step = hid // 4
        at = (2 * c + x) * step
        up_piece = after(lax.dynamic_slice_in_dim(w_up, at, step, axis=1), mine[1])
        down_piece = after(lax.dynamic_slice_in_dim(w_down, at, step, axis=0), mine[2])
        ups, downs = [swap(up_piece, "h")], [swap(down_piece, "h")]
        for part in (ups, downs):
            part.append(swap(part[0], 1))
            part[:0] = [swap(part[0], 0), swap(part[1], 0)]

        qkv2, ctx2, lse2, w2 = [], [], [], []
        for p in range(pairs):
            bias3 = jnp.concatenate(
                (
                    bias_oth[0, p * PAIR : (p + 1) * PAIR],
                    jnp.zeros((PAIR,), F32),
                    bias_oth[1, p * PAIR : (p + 1) * PAIR],
                )
            )
            got = call(
                pair_kernel,
                [((SEQ, 3 * PAIR), BF), ((SEQ, PAIR), BF), ((8, SEQ), F32), ((d, 3 * PAIR), BF)],
                (core, n1, seg, pad, mine[p], rest[p], row(bias3)),
                flops=4e9,
                scratch=[square],
                prefetch=1,
            )
            for keep, value in zip((qkv2, ctx2, lse2, w2), got):
                keep.append(value)
        ctx2, wo2, hidden, n2 = call(
            functools.partial(hidden_kernel, pairs),
            [((SEQ, half), BF), ((half, d), BF), ((SEQ, d), F32), ((SEQ, d), BF)],
            (core, tokens, ctx1, *ctx2, w_out, out_mine, out_rest, row(b_out), row(gain_two),
             row(shift_two)),
            flops=4e9,
            prefetch=1,
        )
        bu1 = lax.dynamic_slice_in_dim(b_up, y * hid, hid)
        bu2 = lax.dynamic_slice_in_dim(b_up, (1 - y) * hid, hid)
        o1, u1, gus1, guk1, gds1, gdk1, gb1 = feed(where, n2, dn, row(bu1), (w_up, w_down))
        gus1r, gds1r = swap(gus1, 0), swap(gds1, 0)
        o2, u2, gus2, guk2, gds2, gdk2, gb2 = feed(
            where, n2, dn, row(bu2), (*ups, *downs), (o1, u1)
        )
        gus2r, gds2r = swap(gus2, 0), swap(gds2, 0)
        output, grad_hidden, small2, gc1, gc2, go1, go2 = call(
            middle_kernel,
            [((SEQ, d), BF), ((SEQ, d), F32), ((8, d), F32)]
            + [((SEQ, half), BF)] * 2
            + [((half, d), BF)] * 2,
            (hidden, o2, u2, dn, row(b_down), row(gain_two), ctx1, ctx2, w_out, wo2),
            flops=6e9,
        )
        order_y = ("h",) + levels
        order_x = levels[:1] + ("h",) + levels[1:]
        sum_up = Sum(plus(guk1, gus1r), plus(guk2, gus2r), order_y)
        sum_down = Sum(plus(gdk1, gds1r), plus(gdk2, gds2r), order_x)
        back_outs = [((d // 2 + half // 3, 3 * half), BF)] * 2 + [((1, 3 * half), F32)]
        back_scratch = [square, pltpu.VMEM((SEQ, 3 * half), BF)]
        gws2, gwk2, sums2, dn1 = call(
            functools.partial(qkv_back_kernel, half, False),
            back_outs + [((SEQ, d), F32)],
            (core, n1, after(gc2, sum_up.own, sum_up.oth, sum_down.own, sum_down.oth), go2, seg,
             pad, *qkv2, *lse2, *w2),
            flops=11e9,
            scratch=back_scratch + [pltpu.VMEM((d, 3 * half), BF)],
            prefetch=1,
        )
        gws2r = swap(gws2, 0)
        first = sum_up.run(1), sum_down.run(1)
        gws1, gwk1, sums1, grad_tokens, small1 = call(
            functools.partial(qkv_back_kernel, half, True),
            back_outs + [((SEQ, d), F32), ((8, d), F32)],
            (core, n1, after(gc1, *first), go1, seg, pad, qkv1, lse1, w_query, w_key, w_value, dn1,
             tokens, grad_hidden, row(gain_one)),
            flops=12e9,
            scratch=back_scratch,
            prefetch=1,
        )
        gws1r = swap(gws1, 0)
        qkv_own, qkv_oth = plus(gwk1, gws1r), plus(gwk2, gws2r)
        cut = qkv_own.shape[0] // 2
        sum_a = Sum(qkv_own[:cut], qkv_oth[:cut], order_y)
        sum_b = Sum(qkv_own[cut:], qkv_oth[cut:], order_x)

        def absolute(own, oth):
            return jnp.where(y == 0, jnp.concatenate((own, oth)), jnp.concatenate((oth, own)))

        sums1, sums2 = sums1[0], sums2[0]
        small = [
            small1[0],
            small1[1],
            small2[2],
            small2[0],
            small2[1],
            small2[3],
            absolute(gb1[0], gb2[0]),
            absolute(sums1[:half], sums2[:half]),
            absolute(sums1[2 * half :], sums2[2 * half :]),
        ]
        packed = jnp.concatenate(small).reshape(-1, 128)
        for level in (0, "h") + levels:
            packed = packed + swap(packed, level)
        packed = packed.reshape(-1)

        up_lo, up_hi = sum_up.finish()
        down_lo, down_hi = sum_down.finish()
        a_lo, a_hi = sum_a.finish()
        b_lo, b_hi = sum_b.finish()
        lo, hi = jnp.concatenate((a_lo, b_lo), axis=0), jnp.concatenate((a_hi, b_hi), axis=0)
        grad_qkv = jnp.concatenate((lo[: d // 2], hi[: d // 2]), axis=0).astype(F32)

        def unpack_out(part):
            flat = part[d // 2 :]
            n = half
            tall = jnp.concatenate([flat[:, k * n : (k + 1) * n] for k in range(3)], axis=0)
            return jnp.concatenate((tall[: half // 2], tall[half // 2 :]), axis=1)

        grad_w_out = jnp.concatenate((unpack_out(lo), unpack_out(hi)), axis=0).astype(F32)
        parts, start = [], 0
        for s in small:
            parts.append(packed[start : start + s.shape[0]])
            start += s.shape[0]
        gg1, gs1, gbo, gg2, gs2, gbd, gbu, gbq, gbv = parts
        return (
            output,
            grad_tokens,
            gg1,
            gs1,
            grad_qkv[:, :half],
            lax.dynamic_slice_in_dim(gbq, y * half, half),
            grad_qkv[:, half : 2 * half],
            grad_qkv[:, 2 * half :],
            lax.dynamic_slice_in_dim(gbv, y * half, half),
            grad_w_out,
            gbo,
            gg2,
            gs2,
            jnp.concatenate((up_lo, up_hi), axis=1).astype(F32),
            gbu,
            jnp.concatenate((down_lo, down_hi), axis=0).astype(F32),
            gbd,
        )

    return per_device


def solution(mesh):
    rows, heads = P(("dp", "head"), None), P("head")
    columns, lines = P(None, "head"), P("head", None)
    in_specs = (
        rows, P("dp"), P("dp"), rows, P(), P(), columns, heads, columns, columns, heads,
        lines, P(), P(), P(), columns, P(), lines, P(),
    )
    out_specs = (
        rows, rows, P(), P(), columns, heads, columns, columns, heads, lines, P(), P(), P(),
        columns, P(), lines, P(),
    )
    return jax.shard_map(
        make_per_device(mesh.shape["dp"]),
        mesh=mesh,
        in_specs=in_specs,
        out_specs=out_specs,
        check_vma=False,
    )
```

```python
import functools
import types

import jax
import jax.numpy as jnp
from jax import lax
from jax.experimental import pallas as pl
from jax.experimental.pallas import tpu as pltpu
from jax.sharding import PartitionSpec as P

HD = 64
SEQ = 512
PAIR = 2 * HD
BLOCK = 512
epsilon = 1e-06
BF = jnp.bfloat16
F32 = jnp.float32
VMEM_LIMIT = 30 * 1024 * 1024


def mm(a, b):
    return lax.dot_general(a, b, (((1,), (0,)), ((), ())), preferred_element_type=F32)


def nt(a, b):
    return lax.dot_general(a, b, (((1,), (1,)), ((), ())), preferred_element_type=F32)


def tn(a, b):
    return lax.dot_general(a, b, (((0,), (0,)), ((), ())), preferred_element_type=F32)


class Input:
    def __init__(self, hbm, vmem, sem):
        self.hbm, self.vmem, self.sem = hbm, vmem, sem
        self.pending = []

    def fetch(self, pairs=None):
        for k, (src, dst) in enumerate(pairs or [(self.hbm, self.vmem)]):
            copy = pltpu.make_async_copy(src, dst, self.sem.at[k])
            copy.start()
            self.pending.append(copy)

    def __call__(self):
        for copy in self.pending:
            copy.wait()
        self.pending = []
        return self.vmem


class Output:
    def __init__(self, ref, buffer, sem):
        self.hbm, self.vmem, self.sem = ref, ref if buffer is None else buffer, sem
        self.stored, self.pending = buffer is not None, []

    def send(self, pairs=None):
        if not self.stored:
            return
        for src, dst in pairs or [(self.vmem, self.hbm)]:
            copy = pltpu.make_async_copy(src, dst, self.sem.at[len(self.pending)])
            copy.start()
            self.pending.append(copy)

    def finish(self):
        for copy in self.pending:
            copy.wait()


class Lazy:
    def __init__(self, value):
        self.value, self.shape = value, value.shape


class Manual:
    def __init__(self, value, shape=None):
        self.value, self.shape = value, shape


class Free:
    def __init__(self, value):
        self.value, self.shape = value, None


class Stored:
    def __init__(self, spec, shape=None):
        self.spec, self.shape = spec, shape or spec[0]


def call(body, scalars, args, outs, scratch=(), copies=8, micros=1):
    names, results = list(args), list(outs)
    kinds = list(args.values())
    values = [k.value if isinstance(k, (Lazy, Manual, Free)) else k for k in kinds]
    stored = [isinstance(k, Stored) for k in outs.values()]
    specs = [k.spec if isinstance(k, Stored) else k for k in outs.values()]
    apart = [isinstance(k, (Lazy, Manual)) for k in kinds]

    def kernel(scalar_ref, *refs):
        n, m = len(names), len(results)
        rest = list(refs[n + m :])
        vm = [rest.pop(0) if a and k.shape else refs[i] for i, (a, k) in enumerate(zip(apart, kinds))]
        vo = [rest.pop(0) if a else None for a in stored]
        sem_in, sem_out, *extra = rest
        ins = [Input(refs[i], vm[i], sem_in.at[i]) for i in range(n)]
        for ref, kind in zip(ins, kinds):
            if isinstance(kind, Lazy):
                ref.fetch()
        out = [Output(refs[n + i], vo[i], sem_out.at[i]) for i in range(m)]
        body(
            scalar_ref,
            types.SimpleNamespace(**dict(zip(names, ins))),
            types.SimpleNamespace(**dict(zip(results, out))),
            *extra,
        )
        for o in out:
            o.finish()

    anywhere = pl.BlockSpec(memory_space=pltpu.HBM)
    whole = lambda shape: pl.BlockSpec(shape, lambda i, s: (0,) * len(shape))
    buffers = [pltpu.VMEM(k.shape, v.dtype) for a, k, v in zip(apart, kinds, values) if a and k.shape]
    buffers += [pltpu.VMEM(k.shape, k.spec[1]) for k in outs.values() if isinstance(k, Stored)]
    buffers += [
        pltpu.SemaphoreType.DMA((len(names), 8)),
        pltpu.SemaphoreType.DMA((len(results), copies)),
    ]
    got = pl.pallas_call(
        kernel,
        grid_spec=pltpu.PrefetchScalarGridSpec(
            num_scalar_prefetch=1,
            grid=(1,),
            in_specs=[anywhere if a else whole(v.shape) for a, v in zip(apart, values)],
            out_specs=[anywhere if a else whole(t[0]) for a, t in zip(stored, specs)],
            scratch_shapes=buffers + list(scratch),
        ),
        out_shape=[(pltpu.HBM if a else pltpu.VMEM)(*t) for a, t in zip(stored, specs)],
        compiler_params=pltpu.CompilerParams(vmem_limit_bytes=VMEM_LIMIT),
        cost_estimate=pl.CostEstimate(flops=int(micros * 0.02e9), bytes_accessed=1000, transcendentals=0),
    )(
        scalars,
        *(
            v if isinstance(k, Free) else pltpu.with_memory_space_constraint(v, pltpu.HBM if a else pltpu.VMEM)
            for a, k, v in zip(apart, kinds, values)
        ),
    )
    return types.SimpleNamespace(**dict(zip(results, got)))


GAIN1, SHIFT1, B_OUT, GAIN2, SHIFT2, B_DOWN, B_QV, SEG, PAD, B_UP = range(10)
VEC_ROWS = 16
G_QV, G_UP = 6, 8


def norm_parts(v):
    centre = jnp.mean(v, axis=-1, keepdims=True)
    shifted = v - centre
    spread = jnp.mean(shifted * shifted, axis=-1, keepdims=True)
    r = lax.rsqrt(spread + epsilon)
    return shifted * r, r


def norm_back(e, xhat, r, gain):
    eg = e * gain
    mean_eg = jnp.mean(eg, axis=-1, keepdims=True)
    return r * (eg - mean_eg - xhat * jnp.mean(eg * xhat, axis=-1, keepdims=True))


def column(row):
    return jnp.transpose(jnp.broadcast_to(row, (128, row.shape[1])))[:, :1]


def fill_bias(vec, bias_ref):
    seg = vec[SEG : SEG + 1, :SEQ]
    seg_col, pad_col = column(seg), column(vec[PAD : PAD + 1, :SEQ])
    for b in range(SEQ // BLOCK):
        cols = slice(b * BLOCK, (b + 1) * BLOCK)
        key = lax.broadcasted_iota(jnp.int32, (SEQ, BLOCK), 0)
        query = lax.broadcasted_iota(jnp.int32, (SEQ, BLOCK), 1) + b * BLOCK
        ok = (seg_col == seg[:, cols]) & ((pad_col == 0) | (key == query))
        bias_ref[:, cols] = jnp.where(ok, 0.0, -1e30)


def attend_pair(q2, k2, v2, bias_ref, lse_ref, at):
    lane = lax.broadcasted_iota(jnp.int32, (SEQ, PAIR), 1)
    row = lax.broadcasted_iota(jnp.int32, (PAIR, SEQ), 0)
    q2 = q2 * BF(HD**-0.5)
    vt = jnp.transpose(v2)
    found = []
    for b in range(SEQ // BLOCK):
        rows = slice(b * BLOCK, (b + 1) * BLOCK)
        total = None
        for e in range(2):
            qe = jnp.where((lane[rows] // HD) == e, q2[rows], BF(0))
            s = nt(k2, qe) + bias_ref[:, rows]
            top = jnp.max(s, axis=0, keepdims=True)
            raised = jnp.exp(s - top)
            den = jnp.sum(raised, axis=0, keepdims=True)
            low = (raised * (1.0 / den)).astype(BF)
            ve = jnp.where((row // HD) == e, vt, BF(0))
            part = mm(ve, low)
            total = part if total is None else total + part
            lse_ref[at + e : at + e + 1, rows] = top + jnp.log(den)
        found.append(jnp.transpose(total).astype(BF))
    return jnp.concatenate(found, axis=0)


def pack_body(d, half, relayed, s, ins, out, buf):
    c, x = s[0], s[3]
    w = [ref.hbm for ref in (ins.wq, ins.wk, ins.wv)]
    d2, q = d // 2, half // 2
    mine = pl.ds(pl.multiple_of(c * d2, d2), d2)
    for m, ref in enumerate((ins.wq, ins.wk, ins.wv)):
        ref.fetch(
            [
                (
                    w[m].at[mine, p * PAIR : (p + 1) * PAIR],
                    buf.at[:d2, (3 * p + m) * PAIR : (3 * p + m + 1) * PAIR],
                )
                for p in range(half // PAIR)
            ]
        )
    ins.wo.fetch(
        [
            (
                ins.wo.hbm.at[pl.ds(pl.multiple_of(c * q, q) + row, n), side * half : (side + 1) * half],
                buf.at[d2 + at : d2 + at + n, k * half : (k + 1) * half],
            )
            for row, n, side, at, k in cuts(q)
        ]
    )
    for ref in (ins.wq, ins.wk, ins.wv):
        ref()
    part = relayed // 2
    out.r.send([(buf.at[pl.ds(pl.multiple_of(x * part, part), part)], out.r.hbm)])
    ins.wo()
    out.p.send([(buf.at[relayed:], out.p.hbm)])


def cuts(q):
    cut, found = 2 * q // 3, []
    for k in range(3):
        row = k * cut
        while row < (k + 1) * cut:
            side = row // q
            n = min((k + 1) * cut, (side + 1) * q) - row
            found.append((row - side * q, n, side, row - k * cut, k))
            row += n
    return found


def first_body(half, s, ins, out, bias_ref):
    vec = ins.vec()
    xhat, _ = norm_parts(ins.tok()[...].astype(F32))
    n1 = (xhat * vec[GAIN1 : GAIN1 + 1] + vec[SHIFT1 : SHIFT1 + 1]).astype(BF)
    out.n1.vmem[...] = n1
    out.n1.send()
    out.vec.vmem[...] = vec[...]
    qkv_ref, ctx_ref, lse_ref = out.qkv.vmem, out.ctx.vmem, out.lse.vmem
    bqv = vec[B_QV : B_QV + 1]
    qkv_ref[:, :half] = (mm(n1, ins.wq()[...]) + bqv[:, :half]).astype(BF)
    qkv_ref[:, half : 2 * half] = mm(n1, ins.wk()[...]).astype(BF)
    qkv_ref[:, 2 * half :] = (mm(n1, ins.wv()[...]) + bqv[:, half:]).astype(BF)
    out.qkv.send()
    fill_bias(vec, bias_ref)
    for p in range(half // PAIR):
        parts = (qkv_ref[:, m * half + p * PAIR : m * half + (p + 1) * PAIR] for m in range(3))
        ctx_ref[:, p * PAIR : (p + 1) * PAIR] = attend_pair(*parts, bias_ref, lse_ref, 2 * p)
    out.ctx.send()
    out.lse.send()
    keep = column(1.0 - vec[PAD : PAD + 1, :SEQ])
    out.dn.vmem[...] = (ins.cot()[...].astype(F32) * keep).astype(BF)
    out.dn.send()


def second_body(half, s, ins, out, bias_ref, w_ref):
    d = w_ref.shape[0]
    d2, q = d // 2, half // 2
    c = s[0]
    wo2 = out.wo2.vmem
    x = s[3]
    for direct, halves, b in ((ins.mine, (ins.r, ins.rx), c), (ins.rest, (ins.rc, ins.rcx), 1 - c)):
        part = halves[0].hbm.shape[0]
        skip = 2 * part
        for ref, bit in zip(halves, (x, 1 - x)):
            rows = pl.ds(pl.multiple_of(b * d2 + bit * part, part // 2), part)
            ref.fetch([(ref.hbm, w_ref.at[rows])])
        src = direct.hbm
        left = d2 - skip
        pairs = [(src.at[:left], w_ref.at[pl.ds(pl.multiple_of(b * d2, d2) + skip, left)])]
        for row, n, side, at, k in cuts(q):
            rows = pl.ds(pl.multiple_of(b * q, q) + row, n)
            pairs.append(
                (src.at[left + at : left + at + n, k * half : (k + 1) * half], wo2.at[rows, side * half : (side + 1) * half])
            )
        direct.fetch(pairs)
    vec = ins.vec()
    fill_bias(vec, bias_ref)
    bqv = ins.other()[B_QV : B_QV + 1]
    bias = []
    for p in range(half // PAIR):
        bias += [bqv[:, p * PAIR : (p + 1) * PAIR], jnp.zeros((1, PAIR), F32)]
        bias += [bqv[:, half + p * PAIR : half + (p + 1) * PAIR]]
    n1 = ins.n1()
    for ref in (ins.mine, ins.rest, ins.r, ins.rx, ins.rc, ins.rcx):
        ref()
    out.w.send([(w_ref, out.w.hbm)])
    out.wo2.send()
    z = (mm(n1[...], w_ref[...]) + jnp.concatenate(bias, axis=1)).astype(BF)
    out.qkv.vmem[...] = z
    out.qkv.send()
    ctx2 = out.ctx2.vmem
    for p in range(half // PAIR):
        parts = (z[:, (3 * p + m) * PAIR : (3 * p + m + 1) * PAIR] for m in range(3))
        ctx2[:, p * PAIR : (p + 1) * PAIR] = attend_pair(*parts, bias_ref, out.lse.vmem, 2 * p)
    out.ctx2.send()
    out.lse.send()
    hidden = ins.tok()[...].astype(F32) + vec[B_OUT : B_OUT + 1]
    hidden = hidden + (mm(ins.ctx1()[...], ins.wo1()[...]) + mm(ctx2[...], wo2[...]))
    out.hid.vmem[...] = hidden
    out.hid.send()
    xhat, _ = norm_parts(hidden)
    n2 = (xhat * vec[GAIN2 : GAIN2 + 1] + vec[SHIFT2 : SHIFT2 + 1]).astype(BF)
    for k, ref in enumerate((out.na, out.nb)):
        ref.vmem[...] = n2[k * SEQ // 2 : (k + 1) * SEQ // 2]
        ref.send()


def feed_body(own, first, s, ins, out):
    y = s[1]
    wu_ref, wd_ref = ins.wu, ins.wd
    d = ins.na.hbm.shape[1]
    rows = out.act.vmem.shape[0]
    n2, wu, wd = ins.na.vmem, wu_ref.vmem, wd_ref.vmem
    ins.na.fetch([(ins.na.hbm, n2.at[: SEQ // 2])])
    if own:
        ins.nb.fetch([(ins.nb.hbm, n2.at[SEQ // 2 :])])
    wu_ref.fetch([(wu_ref.hbm.at[:, k * d : (k + 1) * d], wu.at[k]) for k in range(2)])
    ins.dn.fetch([(ins.dn.hbm.at[first : first + rows], ins.dn.vmem)])
    wd_ref.fetch([(wd_ref.hbm.at[k * d : (k + 1) * d], wd.at[k]) for k in range(2)])
    waits_u, waits_d = wu_ref.pending, wd_ref.pending
    vec = ins.vec()
    ins.na()
    if own:
        ins.nb()
    dn = ins.dn()
    act, gg = out.act.vmem, out.gg.vmem
    for k in range(2):
        cols = slice(k * d, (k + 1) * d)
        waits_u[k].wait()
        gate = mm(n2[...], wu[k]) + vec[pl.ds(B_UP + 2 * y + k, 1), :]
        waits_d[k].wait()
        dact = nt(dn[...], wd[k])
        cdf = 0.5 * (1.0 + lax.erf(gate * (0.5**0.5)))
        pdf = jnp.exp(gate * gate * -0.5) * 0.3989422804014327
        act[:, cols] = (gate * cdf).astype(BF)
        gg[:, cols] = (dact * (cdf + gate * pdf)).astype(BF)
    out.act.send()
    out.gg.send()
    kind = F32 if own else BF
    out.u.vmem[...] = (nt(gg[:, :d], wu[0]) + nt(gg[:, d:], wu[1])).astype(kind)
    out.u.send()
    out.o.vmem[...] = (mm(act[:, :d], wd[0]) + mm(act[:, d:], wd[1])).astype(kind)
    out.o.send()


def feed_grads_body(s, ins, out, n2, dn, act, gg):
    c = s[0]
    d = n2.shape[1]
    early = ((ins.gg1, ins.gg2, ins.gg3, gg), (ins.na, ins.nb, ins.nc, ins.nd, n2))
    late = ((ins.act1, ins.act2, ins.act3, act), (ins.dn1, ins.dn2, dn))
    for *parts, to in early + late:
        at = 0
        for ref in parts:
            rows = ref.hbm.shape[0]
            ref.fetch([(ref.hbm, to.at[at : at + rows])])
            at += rows
    hold = out.uk.hbm.shape
    n, r2 = hold[0], hold[1]
    r = r2 // 2
    for *parts, _ in early:
        for ref in parts:
            ref()
    gu, gd = out.uk.vmem, out.dk.vmem
    for k in range(2):
        cols = slice(k * d, (k + 1) * d)
        gu[k] = tn(n2[...], gg[:, cols]).astype(BF).reshape(n, 2, r, d)
        for to, b in ((out.us, 1 - c), (out.uk, c)):
            to.send([(gu.at[k, :, b], to.hbm.at[:, k * r : (k + 1) * r])])
    for *parts, _ in late:
        for ref in parts:
            ref()
    for k in range(2):
        cols = slice(k * d, (k + 1) * d)
        gd[k] = tn(act[:, cols], dn[...]).astype(BF).reshape(n // 2, 2, r2, d)
        for to, b in ((out.ds, 1 - c), (out.dk, c)):
            to.send([(gd.at[k, :, b], to.hbm.at[k * n // 2 : (k + 1) * n // 2])])
        out.gb.vmem[k : k + 1] = jnp.sum(gg[:, cols].astype(F32), axis=0, keepdims=True)


def middle_body(s, ins, out):
    vec = ins.vec()
    hidden = ins.hid()[...]
    xhat, r = norm_parts(hidden)
    e = ins.u1()[...] + jnp.concatenate((ins.ua()[...], ins.ub()[...]), axis=0).astype(F32)
    dn = ins.dn()[...].astype(F32)
    grad_hidden = dn + norm_back(e, xhat, r, vec[GAIN2 : GAIN2 + 1])
    out.gh.vmem[...] = grad_hidden
    out.gh.send()
    ag = grad_hidden.astype(BF)
    out.gc2.vmem[...] = nt(ag, ins.wo2()[...]).astype(BF)
    out.gc2.send()
    out.gc1.vmem[...] = nt(ag, ins.wo1()[...]).astype(BF)
    out.gc1.send()
    out.go2.vmem[...] = tn(ins.ctx2()[...], ag).astype(BF)
    out.go2.send()
    out.go1.vmem[...] = tn(ins.ctx1()[...], ag).astype(BF)
    out.go1.send()
    small = out.small.vmem
    small[GAIN2 : GAIN2 + 1] = jnp.sum(e * xhat, axis=0, keepdims=True)
    small[SHIFT2 : SHIFT2 + 1] = jnp.sum(e, axis=0, keepdims=True)
    small[B_OUT : B_OUT + 1] = jnp.sum(ag.astype(F32), axis=0, keepdims=True)
    small[B_DOWN : B_DOWN + 1] = jnp.sum(dn, axis=0, keepdims=True)
    out.small.send()


def attend_pair_back(q2, k2, v2, g2, bias_ref, lse_ref, at):
    lane = lax.broadcasted_iota(jnp.int32, (SEQ, PAIR), 1)
    row = lax.broadcasted_iota(jnp.int32, (PAIR, SEQ), 0)
    q2 = q2 * BF(HD**-0.5)
    kt = jnp.transpose(k2)
    dq, dk, dv = [], None, None
    for b in range(SEQ // BLOCK):
        rows = slice(b * BLOCK, (b + 1) * BLOCK)
        dqt = None
        for e in range(2):
            on = (lane[rows] // HD) == e
            qe = jnp.where(on, q2[rows], BF(0))
            ge = jnp.where(on, g2[rows], BF(0))
            ke = jnp.where((row // HD) == e, kt, BF(0))
            s = nt(k2, qe) + bias_ref[:, rows]
            probs = jnp.exp(s - lse_ref[at + e : at + e + 1, rows])
            gp = nt(v2, ge)
            delta = jnp.sum(gp * probs, axis=0, keepdims=True)
            gs = (probs * (gp - delta)).astype(BF)
            t = mm(probs.astype(BF), ge)
            dv = t if dv is None else dv + t
            t = mm(gs, qe)
            dk = t if dk is None else dk + t
            t = mm(ke, gs)
            dqt = t if dqt is None else dqt + t
        dq.append((jnp.transpose(dqt) * (HD**-0.5)).astype(BF))
    return jnp.concatenate(dq, axis=0), dk.astype(BF), dv.astype(BF)


def weight_grads(c, ins, out, gw, half):
    d2, q = gw.shape[0] // 2, half // 2
    go = ins.go()
    for dst, b in ((out.gws, 1 - c), (out.gwk, c)):
        dst.send([(gw.at[pl.ds(pl.multiple_of(b * d2, d2), d2)], dst.hbm.at[:d2])])
        for row, n, side, at, k in cuts(q):
            src = go.at[pl.ds(pl.multiple_of(b * q, q) + row, n), side * half : (side + 1) * half]
            dst.send([(src, dst.hbm.at[d2 + at : d2 + at + n, k * half : (k + 1) * half])])


def other_back_body(half, s, ins, out, bias_ref, gw):
    grad_ref = out.grad.vmem
    fill_bias(ins.vec(), bias_ref)
    for p in range(half // PAIR):
        at = [slice(m * half + p * PAIR, m * half + (p + 1) * PAIR) for m in range(3)]
        local = [slice((3 * p + m) * PAIR, (3 * p + m + 1) * PAIR) for m in range(3)]
        parts = [ins.qkv()[:, local[m]] for m in range(3)]
        grads = attend_pair_back(*parts, ins.gc()[:, at[0]], bias_ref, ins.lse(), 2 * p)
        for m in range(3):
            grad_ref[:, at[m]] = grads[m]
    out.grad.send()
    gw[...] = tn(ins.n1()[...], grad_ref[...]).astype(BF)
    weight_grads(s[0], ins, out, gw, half)


def own_back_body(half, s, ins, out, bias_ref, gw):
    grad_ref = out.grad.vmem
    fill_bias(ins.vec(), bias_ref)
    for p in range(half // PAIR):
        at = [slice(m * half + p * PAIR, m * half + (p + 1) * PAIR) for m in range(3)]
        parts = [ins.qkv()[:, at[m]] for m in range(3)]
        grads = attend_pair_back(*parts, ins.gc()[:, at[0]], bias_ref, ins.lse(), 2 * p)
        for m in range(3):
            grad_ref[:, at[m]] = grads[m]
    out.grad.send()
    gw[...] = tn(ins.n1()[...], grad_ref[...]).astype(BF)
    weight_grads(s[0], ins, out, gw, half)


def last_body(half, s, ins, out, w_ref):
    vec = ins.vec()
    y = s[1]
    mine, theirs = ins.grad1(), ins.grad2()
    e = None
    for m, w in enumerate((ins.wq, ins.wk, ins.wv)):
        t = nt(mine[:, m * half : (m + 1) * half], w()[...])
        e = t if e is None else e + t
    w = ins.w()
    for p in range(half // PAIR):
        for m in range(3):
            at = slice(m * half + p * PAIR, m * half + (p + 1) * PAIR)
            w_ref[:, at] = w[:, (3 * p + m) * PAIR : (3 * p + m + 1) * PAIR]
    e = e + nt(theirs[...], w_ref[...])
    xhat, r = norm_parts(ins.tok()[...].astype(F32))
    out.small.vmem[...] = jnp.zeros_like(out.small.vmem)
    small = out.small.vmem.at[:, : vec.shape[1]]
    before = ins.small2()
    for k in (GAIN2, SHIFT2, B_OUT, B_DOWN):
        small[k : k + 1] = before[k : k + 1]
    small[GAIN1 : GAIN1 + 1] = jnp.sum(e * xhat, axis=0, keepdims=True)
    small[SHIFT1 : SHIFT1 + 1] = jnp.sum(e, axis=0, keepdims=True)
    sums = [jnp.sum(v[...].astype(F32), axis=0, keepdims=True) for v in (mine, theirs)]
    for k in range(2):
        a, b = (v[:, 2 * k * half : (2 * k + 1) * half] for v in sums)
        both = jnp.where(y == 0, jnp.concatenate((a, b), axis=1), jnp.concatenate((b, a), axis=1))
        small[G_QV + k : G_QV + k + 1] = both
    gb = ins.gb()
    for k in range(2):
        small[pl.ds(G_UP + 2 * y + k, 1), :] = gb[k : k + 1]
    out.small.send()
    out.gt.vmem[...] = ins.gh()[...] + norm_back(e, xhat, r, vec[GAIN1 : GAIN1 + 1])
    out.gt.send()


def output_body(s, ins, out):
    bias = ins.vec()[B_DOWN : B_DOWN + 1]
    res = ins.hid()[...] + (ins.o1()[...] + ins.o2()[...].astype(F32)) + bias
    out.out.vmem[...] = res.astype(BF)
    out.out.send()


def place(s, refs, order, buf):
    for k, ref in enumerate(refs):
        core, first = s[0] ^ (k >> 1), k & 1
        pairs = []
        for m in range(4):
            at = 0
            for level, bit in zip(order, (first, m >> 1)):
                at = at + (s[2 + level] ^ bit) * (1 << (level - 1))
            at = at + (m & 1) * 4
            pairs.append((ref.hbm.at[m >> 1, m & 1], buf.at[2 * at + core]))
        ref.fetch(pairs)


def results_body(half, order_a, order_b, s, ins, out, up, down, buf):
    z = s[4] + 2 * s[5]
    n, r = buf.shape[1:3]
    refs = (ins.a, ins.b, ins.c, ins.d)
    ups, downs = (ins.u0, ins.u1, ins.u2, ins.u3), (ins.d0, ins.d1, ins.d2, ins.d3)
    place(s, ups, order_a, up)
    for k, ref in enumerate(refs):
        core, x = s[0] ^ (k >> 1), s[3] ^ (k & 1)
        ref.fetch([(ref.hbm.at[m * r : (m + 1) * r], buf.at[core, (z ^ m) * 2 + x]) for m in range(4)])
    place(s, downs, order_b, down)
    i, r2, d = up.shape
    h2 = r2 // 2
    for ref in ups:
        ref()
    to = out.gu.vmem
    for k in range(2):
        part = slice(k * i // 2, (k + 1) * i // 2)
        rows = slice(k * i * h2 // 2, (k + 1) * i * h2 // 2)
        for h in range(2):
            to[rows, h * d : (h + 1) * d] = up[part, h * h2 : (h + 1) * h2].astype(F32).reshape(i * h2 // 2, d)
        out.gu.send([(to.at[rows], out.gu.hbm.at[rows])])
    for ref in refs:
        ref()
    d2, q = half, half // 2
    for c in range(2):
        whole = buf[c].reshape(n * r, buf.shape[3])
        for m, ref in enumerate((out.gq, out.gk, out.gv)):
            ref.vmem[c * d2 : (c + 1) * d2] = whole[:d2, m * half : (m + 1) * half].astype(F32)
            ref.send([(ref.vmem.at[c * d2 : (c + 1) * d2], ref.hbm.at[c * d2 : (c + 1) * d2])])
        for row, size, side, at, k in cuts(q):
            piece = whole[d2 + at : d2 + at + size, k * half : (k + 1) * half]
            out.go.vmem[c * q + row : c * q + row + size, side * half : (side + 1) * half] = piece.astype(F32)
    out.go.send()
    for ref in downs:
        ref()
    to = out.gd.vmem
    for k in range(2):
        part = slice(k * i // 2, (k + 1) * i // 2)
        rows = slice(k * i * r2 // 2, (k + 1) * i * r2 // 2)
        to[rows] = down[part].astype(F32).reshape(i * r2 // 2, d)
        out.gd.send([(to.at[rows], out.gd.hbm.at[rows])])


def make_per_device(dp_size):
    bits = dp_size.bit_length() - 1
    assert dp_size == 1 << bits and bits >= 4
    group = 16
    levels, extra = (1, 2, 3), tuple(range(4, bits))

    def after(value, *others):
        return lax.optimization_barrier((value,) + others)[0]

    def swap(value, level, start=None, until=None):
        if start is not None:
            value = after(value, start)
        if level == "h":
            got = lax.ppermute(value, "head", [(0, 1), (1, 0)])
        else:
            got = lax.ppermute(value, "dp", [(i, i ^ (1 << level)) for i in range(dp_size)])
        return got if until is None else after(got, until)

    def after_all(values, others):
        return lax.optimization_barrier((values, others))[0]

    def tie(kernel, others):
        got, others = lax.optimization_barrier((vars(kernel), others))
        return types.SimpleNamespace(**got), others

    def my_bit(level):
        return (lax.axis_index("dp") >> level) & 1

    def plus(*terms):
        return sum(t.astype(F32) for t in terms).astype(BF)

    def swap_z(values):
        return [
            lax.ppermute(v, "dp", [(i, i ^ (m << 2)) for i in range(dp_size)])
            for m, v in zip((1, 2, 3), values)
        ]

    def cut_x(*terms):
        b = my_bit(1)
        pick = lambda t, k: lax.dynamic_index_in_dim(t, k, 1, keepdims=False)
        return plus(*(pick(t, 1 - b) for t in terms)), plus(*(pick(t, b) for t in terms))

    def cut_z(*terms):
        z = (lax.axis_index("dp") >> 2) & 3
        pick = lambda t, k: lax.dynamic_index_in_dim(t, k, 0, keepdims=False)
        return [plus(*(pick(t, z ^ m) for t in terms)) for m in (1, 2, 3, 0)]

    class Part:
        def __init__(self, *terms, cut=True):
            self.terms = [t.reshape((2, 2, 2, -1, t.shape[-1])) for t in terms] if cut else list(terms)
            self.left, self.gathering = list(levels[::-1]), False

        def wait(self, until):
            self.terms[-1] = after(self.terms[-1], until)

        def step(self, level, until=None):
            axis = self.left.index(level)
            self.left.remove(level)
            b = my_bit(level)
            pick = lambda t, k: lax.dynamic_index_in_dim(t, k, axis, keepdims=False)
            sent = plus(*(pick(t, 1 - b) for t in self.terms))
            kept = plus(*(pick(t, b) for t in self.terms))
            self.terms = [kept, swap(sent, level, until=until)]
            return sent

        def widen(self, level):
            mine = self.value()
            self.terms = [mine, swap(mine, level)]

        def value(self):
            if self.gathering and len(self.terms) > 1:
                self.terms = [jnp.stack(self.terms)]
            if len(self.terms) > 1:
                self.terms = [plus(*self.terms)]
            return self.terms[0]

    def per_device(
        tokens, segments, padding, cotangent, gain_one, shift_one, w_query, b_query, w_key,
        w_value, b_value, w_out, b_out, gain_two, shift_two, w_up, b_up, w_down, b_down,
    ):
        rows, d = tokens.shape
        assert rows == SEQ
        y, dp = lax.axis_index("head"), lax.axis_index("dp")
        half, hid = w_query.shape[1], w_up.shape[1]
        rows_c = d // 2 + half // 3
        r = d // group
        scalars = jnp.stack((dp & 1, y, dp, (dp >> 1) & 1, (dp >> 2) & 1, (dp >> 3) & 1))
        scalars = scalars.astype(jnp.int32)
        line = lambda v: jnp.pad(
            lax.dynamic_slice_in_dim(v, y * rows, rows).astype(F32), (0, d - rows)
        )
        vec = jnp.concatenate(
            (gain_one, shift_one, b_out, gain_two, shift_two, b_down, b_query, b_value,
             line(segments), line(padding), b_up, jnp.zeros((VEC_ROWS * d - 9 * d - 2 * hid,), F32))
        ).reshape(VEC_ROWS, d)
        square = pltpu.VMEM((SEQ, SEQ), F32)
        act, wide, part = ((SEQ, d), BF), ((SEQ, d), F32), ((SEQ, half), BF)
        three = ((SEQ, 3 * half), BF)
        lse = ((8, SEQ), F32)
        rows_half = ((SEQ // 2, d), BF)

        relayed = 320
        sent = call(
            functools.partial(pack_body, d, half, relayed), scalars,
            dict(wq=Manual(w_query), wk=Manual(w_key), wv=Manual(w_value), wo=Manual(w_out)),
            dict(r=Stored(((relayed // 2, 3 * half), BF), (8, 128)),
                 p=Stored(((rows_c - relayed, 3 * half), BF), (8, 128))),
            scratch=[pltpu.VMEM((rows_c, 3 * half), BF)],
        )
        one = call(
            functools.partial(first_body, half), scalars,
            dict(vec=Free(vec), tok=Lazy(tokens), wq=Lazy(w_query), wk=Lazy(w_key), wv=Lazy(w_value),
                 cot=Lazy(cotangent)),
            dict(n1=Stored(act), qkv=Stored(three), ctx=Stored(part), lse=Stored(lse), dn=Stored(act),
                 vec=((VEC_ROWS, d), F32)),
            scratch=[square], micros=8,
        )
        one, relay = tie(one, swap(sent.r, "h"))
        n1, dn = one.n1, one.dn
        relay_x, mine, other = swap(relay, 1), swap(sent.p, "h"), swap(vec, "h")
        vec = one.vec
        relay_c = swap(relay, 0)
        relay_x, mine, other = lax.optimization_barrier((relay_x, mine, other))
        dn_oth = swap(dn, "h", start=mine)
        weights = dict(mine=Manual(mine), rest=Manual(swap(mine, 0)), r=Manual(relay), rx=Manual(relay_x),
                       rc=Manual(relay_c), rcx=Manual(swap(relay_x, 0)))
        two = call(
            functools.partial(second_body, half), scalars,
            dict(vec=vec, other=Free(other), n1=Lazy(n1), tok=Lazy(tokens), ctx1=Lazy(one.ctx),
                 wo1=Lazy(w_out), **weights),
            dict(w=Stored(((d, 3 * half), BF), (16, 128)), qkv=Stored(three), lse=Stored(lse),
                 wo2=Stored(((half, d), BF)), ctx2=Stored(part), hid=Stored(wide), na=Stored(rows_half), nb=Stored(rows_half)),
            scratch=[square, pltpu.VMEM((d, 3 * half), BF)], micros=12,
        )
        two, dn_oth = tie(two, dn_oth)

        na, nb = swap(two.na, "h"), swap(two.nb, "h")

        def feed(first, dn, **rows):
            own = first is None
            count = SEQ if own else SEQ // 2
            units = Stored(((count, hid), BF))
            partial = Stored(((count, d), F32 if own else BF))
            at = {k: Manual(v, None if i else (count, d)) for i, (k, v) in enumerate(rows.items())}
            return call(
                functools.partial(feed_body, own, first or 0), scalars,
                dict(vec=vec, dn=Manual(dn, (count, d)), wu=Manual(w_up, (2, d, d)),
                     wd=Manual(w_down, (2, d, d)), **at),
                dict(act=units, gg=units, u=partial, o=partial),
                micros=8,
            )

        f1, na = tie(feed(None, dn, na=two.na, nb=two.nb), na)
        f2 = feed(0, dn_oth, na=na)
        u_a = swap(f2.u, "h")
        f2, nb = tie(f2, nb)
        f3 = feed(SEQ // 2, dn_oth, na=nb)
        f3, u_a = tie(f3, u_a)
        u_b = swap(f3.u, "h")
        eighth = ((group // 2, 2 * r, d), BF)
        fg = call(
            feed_grads_body, scalars,
            dict(gg1=Manual(f1.gg), gg2=Manual(f2.gg), gg3=Manual(f3.gg), na=Manual(two.na), nb=Manual(two.nb),
                 nc=Manual(na), nd=Manual(nb), act1=Manual(f1.act), act2=Manual(f2.act), act3=Manual(f3.act),
                 dn1=Manual(dn), dn2=Manual(dn_oth)),
            dict(us=Stored(eighth, (8, 128)), uk=Stored(eighth, (2, group // 2, 2, r, d)),
                 ds=Stored(eighth, (8, 128)), dk=Stored(eighth, (2, group // 4, 2, 2 * r, d)),
                 gb=((8, d), F32)),
            scratch=[pltpu.VMEM((2 * SEQ, d), BF)] * 2 + [pltpu.VMEM((2 * SEQ, hid), BF)] * 2,
            micros=8,
        )
        fg, u_b = tie(fg, u_b)
        fg, u_b = tie(fg, u_b)
        up = Part(fg.uk, swap(fg.us, 0))
        down = Part(fg.dk, swap(fg.ds, 0))
        first_sent = up.step(1), down.step(2)

        mid = call(
            middle_body, scalars,
            dict(vec=vec, hid=two.hid, u1=f1.u, ua=Lazy(u_a), ub=Lazy(after(u_b, *first_sent)), dn=dn,
                 wo2=two.wo2, wo1=w_out, ctx2=two.ctx2, ctx1=one.ctx),
            dict(gh=Stored(wide), gc2=part, gc1=Stored(part), go2=Stored(((half, d), BF)),
                 go1=Stored(((half, d), BF)), small=((8, d), F32)),
            micros=6,
        )
        mid, (up.terms[-1], down.terms[-1]) = tie(mid, (up.terms[-1], down.terms[-1]))
        second_sent = up.step(2), down.step(1)
        piece = ((rows_c, 3 * half), BF)
        back = dict(
            outs=dict(gws=Stored(piece, (16, 128)), gwk=Stored(piece, (16, 128)), grad=Stored(three)),
            scratch=[square, pltpu.VMEM((d, 3 * half), BF)],
            micros=11,
        )
        o_oth = swap(jnp.concatenate((f2.o, f3.o)), "h", start=mid.gc2)
        b2 = call(
            functools.partial(other_back_body, half), scalars,
            dict(vec=vec, gc=after(mid.gc2, *second_sent), go=Lazy(mid.go2), n1=n1, qkv=two.qkv, lse=two.lse),
            **back,
        )
        b2, (up.terms[-1], down.terms[-1]) = tie(b2, (up.terms[-1], down.terms[-1]))
        grid = lambda v: v.reshape((4, 2, -1, v.shape[-1]))
        oth_sent, oth_kept = cut_x(grid(b2.gwk), grid(swap(b2.gws, 0)))
        ab = plus(*up.terms), plus(*down.terms)
        ab_got = swap(ab[0], 3), swap(ab[1], 3)
        third_sent = *ab, oth_sent
        oth_got = swap(oth_sent, 1)
        b1 = call(
            functools.partial(own_back_body, half), scalars,
            dict(vec=vec, gc=Lazy(mid.gc1), go=Lazy(mid.go1), qkv=Lazy(after(one.qkv, *third_sent)),
                 lse=one.lse, n1=n1),
            **back,
        )
        b1, (oth_got, up_got, o_oth) = tie(b1, (oth_got, ab_got[0], o_oth))
        theirs = plus(oth_kept, oth_got)
        own_c = after_all(swap(b1.gws, 0), theirs)
        theirs = swap(theirs, "h")
        own_sent, own_kept = cut_x(grid(b1.gwk), grid(own_c))
        own_got = swap(own_sent, 1)
        last_sent = (own_sent,)
        last = call(
            functools.partial(last_body, half), scalars,
            dict(vec=vec, grad1=Lazy(after(b1.grad, *last_sent)), grad2=Lazy(b2.grad), wq=w_query,
                 wk=w_key, wv=w_value, tok=tokens, gh=Lazy(mid.gh), small2=mid.small,
                 gb=fg.gb, w=two.w),
            dict(small=((VEC_ROWS, 3 * half), F32), gt=Stored(wide)),
            scratch=[pltpu.VMEM((d, 3 * half), BF)], micros=12,
        )
        last, (own_got, theirs, down_got) = tie(last, (own_got, theirs, ab_got[1]))
        *own_sent, own_kept = cut_z(own_kept, own_got, theirs)
        own_z = swap_z(own_sent)
        ab, ab_got = after_all((ab, (up_got, down_got)), own_sent)
        feed_sums = [plus(p, q) for p, q in zip(ab, ab_got)]
        for level in extra:
            feed_sums = [plus(p, swap(p, level)) for p in feed_sums]
        up, down = (Part(p, cut=False) for p in feed_sums)
        up.gathering = down.gathering = True
        up.widen(1)
        down.widen(2)
        small = after_all(last.small, feed_sums)
        small = small + swap(small, 0)
        small = small + swap(small, "h")
        output = call(
            output_body, scalars,
            dict(vec=vec, hid=Lazy(after_all(two.hid, feed_sums)), o1=Lazy(f1.o), o2=Lazy(o_oth)),
            dict(out=Stored(act)), micros=4,
        )
        output, own_z = tie(output, own_z)
        n = rows_c // 8
        total = plus(own_kept, *own_z)
        for level in extra:
            total = plus(total, swap(total, level))
            small = small + swap(small, level)
        message = jnp.concatenate((total, small.astype(BF)))
        got = swap_z([message] * 3)
        up.terms[-1], down.terms[-1] = after_all((up.terms[-1], down.terms[-1]), message)
        u, d_ = up.value(), down.value()
        u_got, d_got, u_c, d_c = swap(u, 2), swap(d_, 1), swap(u, 0), swap(d_, 0)
        got, u_c, d_c = after_all((got, u_c, d_c), (u, d_))
        small = small + sum(g[n:].astype(F32) for g in got)
        w_all = jnp.concatenate([total] + [g[:n] for g in got] + [small.astype(BF)])
        w_x, w_c = swap(w_all, 1), swap(w_all, 0)
        u_got, d_got = after_all((u_got, d_got), w_all)
        u_got, d_got = after_all((u_got, d_got), w_all)
        w_x, u_cx, d_cx = lax.optimization_barrier((w_x, swap(u_got, 0), swap(d_got, 0)))
        block = Stored(((d, half), F32))
        done = call(
            functools.partial(results_body, half, (2, 1), (1, 2)), scalars,
            dict(u0=Manual(u), u1=Manual(u_got), u2=Manual(u_c), u3=Manual(u_cx),
                 d0=Manual(d_), d1=Manual(d_got), d2=Manual(d_c), d3=Manual(d_cx),
                 a=Manual(w_all), b=Manual(w_x), c=Manual(w_c), d=Manual(swap(w_x, 0))),
            dict(gu=Stored(((d, hid), F32)), gd=Stored(((hid, d), F32)), gq=block, gk=block, gv=block,
                 go=Stored(((half, d), F32))),
            scratch=[pltpu.VMEM((group, 2 * r, d), BF)] * 2 + [pltpu.VMEM((2, 8, n, 3 * half), BF)], micros=9,
        )
        own_bias = lambda v: lax.dynamic_slice_in_dim(v, y * half, half)
        small = (small + w_x[4 * n :].astype(F32))[:, :d]
        vectors = [small[k] for k in (GAIN1, SHIFT1, B_OUT, GAIN2, SHIFT2, B_DOWN)]
        vectors += [own_bias(small[G_QV]), own_bias(small[G_QV + 1]), small[G_UP : G_UP + 4].reshape(-1)]
        gain1, shift1, bo, gain2, shift2, bd, bq, bv, bu = vectors
        return (
            output.out, last.gt, gain1, shift1, done.gq, bq, done.gk, done.gv, bv, done.go,
            bo, gain2, shift2, done.gu, bu, done.gd, bd,
        )

    return per_device


def solution(mesh):
    rows, heads = P(("dp", "head"), None), P("head")
    columns, lines = P(None, "head"), P("head", None)
    in_specs = (
        rows, P("dp"), P("dp"), rows, P(), P(), columns, heads, columns, columns, heads,
        lines, P(), P(), P(), columns, P(), lines, P(),
    )
    out_specs = (
        rows, rows, P(), P(), columns, heads, columns, columns, heads, lines, P(), P(), P(),
        columns, P(), lines, P(),
    )
    return jax.shard_map(
        make_per_device(mesh.shape["dp"]),
        mesh=mesh,
        in_specs=in_specs,
        out_specs=out_specs,
        check_vma=False,
    )
```

```python
import functools
import types

import jax
import jax.numpy as jnp
from jax import lax
from jax.experimental import pallas as pl
from jax.experimental.pallas import tpu as pltpu
from jax.sharding import PartitionSpec as P

HD = 64
SEQ = 512
PAIR = 2 * HD
BLOCK = 512
epsilon = 1e-06
BF = jnp.bfloat16
F32 = jnp.float32
VMEM_LIMIT = 30 * 1024 * 1024


def mm(a, b):
    return lax.dot_general(a, b, (((1,), (0,)), ((), ())), preferred_element_type=F32)


def nt(a, b):
    return lax.dot_general(a, b, (((1,), (1,)), ((), ())), preferred_element_type=F32)


def tn(a, b):
    return lax.dot_general(a, b, (((0,), (0,)), ((), ())), preferred_element_type=F32)


class Input:
    def __init__(self, hbm, vmem, sem):
        self.hbm, self.vmem, self.sem = hbm, vmem, sem
        self.pending = []

    def fetch(self, pairs=None):
        for k, (src, dst) in enumerate(pairs or [(self.hbm, self.vmem)]):
            copy = pltpu.make_async_copy(src, dst, self.sem.at[k])
            copy.start()
            self.pending.append(copy)

    def __call__(self):
        for copy in self.pending:
            copy.wait()
        self.pending = []
        return self.vmem


class Output:
    def __init__(self, ref, buffer, sem):
        self.hbm, self.vmem, self.sem = ref, ref if buffer is None else buffer, sem
        self.stored, self.pending = buffer is not None, []

    def send(self, pairs=None):
        if not self.stored:
            return
        for src, dst in pairs or [(self.vmem, self.hbm)]:
            copy = pltpu.make_async_copy(src, dst, self.sem.at[len(self.pending)])
            copy.start()
            self.pending.append(copy)

    def finish(self):
        for copy in self.pending:
            copy.wait()


class Lazy:
    def __init__(self, value):
        self.value, self.shape = value, value.shape


class Manual:
    def __init__(self, value, shape=None):
        self.value, self.shape = value, shape


class Free:
    def __init__(self, value):
        self.value, self.shape = value, None


class Stored:
    def __init__(self, spec, shape=None):
        self.spec, self.shape = spec, shape or spec[0]


def call(body, scalars, args, outs, scratch=(), copies=8, micros=1):
    names, results = list(args), list(outs)
    kinds = list(args.values())
    values = [k.value if isinstance(k, (Lazy, Manual, Free)) else k for k in kinds]
    stored = [isinstance(k, Stored) for k in outs.values()]
    specs = [k.spec if isinstance(k, Stored) else k for k in outs.values()]
    apart = [isinstance(k, (Lazy, Manual)) for k in kinds]

    def kernel(scalar_ref, *refs):
        n, m = len(names), len(results)
        rest = list(refs[n + m :])
        vm = [rest.pop(0) if a and k.shape else refs[i] for i, (a, k) in enumerate(zip(apart, kinds))]
        vo = [rest.pop(0) if a else None for a in stored]
        sem_in, sem_out, *extra = rest
        ins = [Input(refs[i], vm[i], sem_in.at[i]) for i in range(n)]
        for ref, kind in zip(ins, kinds):
            if isinstance(kind, Lazy):
                ref.fetch()
        out = [Output(refs[n + i], vo[i], sem_out.at[i]) for i in range(m)]
        body(
            scalar_ref,
            types.SimpleNamespace(**dict(zip(names, ins))),
            types.SimpleNamespace(**dict(zip(results, out))),
            *extra,
        )
        for o in out:
            o.finish()

    anywhere = pl.BlockSpec(memory_space=pltpu.HBM)
    whole = lambda shape: pl.BlockSpec(shape, lambda i, s: (0,) * len(shape))
    buffers = [pltpu.VMEM(k.shape, v.dtype) for a, k, v in zip(apart, kinds, values) if a and k.shape]
    buffers += [pltpu.VMEM(k.shape, k.spec[1]) for k in outs.values() if isinstance(k, Stored)]
    buffers += [
        pltpu.SemaphoreType.DMA((len(names), 8)),
        pltpu.SemaphoreType.DMA((len(results), copies)),
    ]
    got = pl.pallas_call(
        kernel,
        grid_spec=pltpu.PrefetchScalarGridSpec(
            num_scalar_prefetch=1,
            grid=(1,),
            in_specs=[anywhere if a else whole(v.shape) for a, v in zip(apart, values)],
            out_specs=[anywhere if a else whole(t[0]) for a, t in zip(stored, specs)],
            scratch_shapes=buffers + list(scratch),
        ),
        out_shape=[(pltpu.HBM if a else pltpu.VMEM)(*t) for a, t in zip(stored, specs)],
        compiler_params=pltpu.CompilerParams(vmem_limit_bytes=VMEM_LIMIT),
        cost_estimate=pl.CostEstimate(flops=int(micros * 0.02e9), bytes_accessed=1000, transcendentals=0),
    )(
        scalars,
        *(
            v if isinstance(k, Free) else pltpu.with_memory_space_constraint(v, pltpu.HBM if a else pltpu.VMEM)
            for a, k, v in zip(apart, kinds, values)
        ),
    )
    return types.SimpleNamespace(**dict(zip(results, got)))


GAIN1, SHIFT1, B_OUT, GAIN2, SHIFT2, B_DOWN, B_QV, SEG, PAD, B_UP = range(10)
VEC_ROWS, SUM_ROWS = 16, 8
G_QV, G_UP = 6, 8


def norm_parts(v):
    centre = jnp.mean(v, axis=-1, keepdims=True)
    shifted = v - centre
    spread = jnp.mean(shifted * shifted, axis=-1, keepdims=True)
    r = lax.rsqrt(spread + epsilon)
    return shifted * r, r


def norm_back(e, xhat, r, gain):
    eg = e * gain
    mean_eg = jnp.mean(eg, axis=-1, keepdims=True)
    return r * (eg - mean_eg - xhat * jnp.mean(eg * xhat, axis=-1, keepdims=True))


def column(row):
    return jnp.transpose(jnp.broadcast_to(row, (128, row.shape[1])))[:, :1]


def fill_bias(vec, bias_ref):
    seg = vec[SEG : SEG + 1, :SEQ]
    seg_col, pad_col = column(seg), column(vec[PAD : PAD + 1, :SEQ])
    for b in range(SEQ // BLOCK):
        cols = slice(b * BLOCK, (b + 1) * BLOCK)
        key = lax.broadcasted_iota(jnp.int32, (SEQ, BLOCK), 0)
        query = lax.broadcasted_iota(jnp.int32, (SEQ, BLOCK), 1) + b * BLOCK
        ok = (seg_col == seg[:, cols]) & ((pad_col == 0) | (key == query))
        bias_ref[:, cols] = jnp.where(ok, 0.0, -1e30)


def attend_pair(q2, k2, v2, bias_ref, lse_ref, at):
    lane = lax.broadcasted_iota(jnp.int32, (SEQ, PAIR), 1)
    row = lax.broadcasted_iota(jnp.int32, (PAIR, SEQ), 0)
    q2 = q2 * BF(HD**-0.5)
    vt = jnp.transpose(v2)
    found = []
    for b in range(SEQ // BLOCK):
        rows = slice(b * BLOCK, (b + 1) * BLOCK)
        total = None
        for e in range(2):
            qe = jnp.where((lane[rows] // HD) == e, q2[rows], BF(0))
            s = nt(k2, qe) + bias_ref[:, rows]
            top = jnp.max(s, axis=0, keepdims=True)
            raised = jnp.exp(s - top)
            den = jnp.sum(raised, axis=0, keepdims=True)
            low = (raised * (1.0 / den)).astype(BF)
            ve = jnp.where((row // HD) == e, vt, BF(0))
            part = mm(ve, low)
            total = part if total is None else total + part
            lse_ref[at + e : at + e + 1, rows] = top + jnp.log(den)
        found.append(jnp.transpose(total).astype(BF))
    return jnp.concatenate(found, axis=0)


def pack_body(d, half, relayed, s, ins, out, buf):
    c, x = s[0], s[3]
    w = [ref.hbm for ref in (ins.wq, ins.wk, ins.wv)]
    d2, q = d // 2, half // 2
    mine = pl.ds(pl.multiple_of(c * d2, d2), d2)
    for m, ref in enumerate((ins.wq, ins.wk, ins.wv)):
        ref.fetch(
            [
                (
                    w[m].at[mine, p * PAIR : (p + 1) * PAIR],
                    buf.at[:d2, (3 * p + m) * PAIR : (3 * p + m + 1) * PAIR],
                )
                for p in range(half // PAIR)
            ]
        )
    ins.wo.fetch(
        [
            (
                ins.wo.hbm.at[pl.ds(pl.multiple_of(c * q, q) + row, n), side * half : (side + 1) * half],
                buf.at[d2 + at : d2 + at + n, k * half : (k + 1) * half],
            )
            for row, n, side, at, k in cuts(q)
        ]
    )
    for ref in (ins.wq, ins.wk, ins.wv):
        ref()
    part = relayed // 2
    out.r.send([(buf.at[pl.ds(pl.multiple_of(x * part, part), part)], out.r.hbm)])
    ins.wo()
    out.p.send([(buf.at[relayed:], out.p.hbm)])


def cuts(q):
    cut, found = 2 * q // 3, []
    for k in range(3):
        row = k * cut
        while row < (k + 1) * cut:
            side = row // q
            n = min((k + 1) * cut, (side + 1) * q) - row
            found.append((row - side * q, n, side, row - k * cut, k))
            row += n
    return found


def first_body(half, s, ins, out, bias_ref):
    vec = ins.vec()
    xhat, _ = norm_parts(ins.tok()[...].astype(F32))
    n1 = (xhat * vec[GAIN1 : GAIN1 + 1] + vec[SHIFT1 : SHIFT1 + 1]).astype(BF)
    out.n1.vmem[...] = n1
    out.n1.send()
    out.vec.vmem[...] = vec[...]
    qkv_ref, ctx_ref, lse_ref = out.qkv.vmem, out.ctx.vmem, out.lse.vmem
    bqv = vec[B_QV : B_QV + 1]
    qkv_ref[:, :half] = (mm(n1, ins.wq()[...]) + bqv[:, :half]).astype(BF)
    qkv_ref[:, half : 2 * half] = mm(n1, ins.wk()[...]).astype(BF)
    qkv_ref[:, 2 * half :] = (mm(n1, ins.wv()[...]) + bqv[:, half:]).astype(BF)
    out.qkv.send()
    fill_bias(vec, bias_ref)
    for p in range(half // PAIR):
        parts = (qkv_ref[:, m * half + p * PAIR : m * half + (p + 1) * PAIR] for m in range(3))
        ctx_ref[:, p * PAIR : (p + 1) * PAIR] = attend_pair(*parts, bias_ref, lse_ref, 2 * p)
    out.ctx.send()
    out.lse.send()
    keep = column(1.0 - vec[PAD : PAD + 1, :SEQ])
    out.dn.vmem[...] = (ins.cot()[...].astype(F32) * keep).astype(BF)
    out.dn.send()


def second_body(half, s, ins, out, bias_ref, w_ref):
    d = w_ref.shape[0]
    d2, q = d // 2, half // 2
    c = s[0]
    wo2 = out.wo2.vmem
    x = s[3]
    for direct, halves, b in ((ins.mine, (ins.r, ins.rx), c), (ins.rest, (ins.rc, ins.rcx), 1 - c)):
        part = halves[0].hbm.shape[0]
        skip = 2 * part
        for ref, bit in zip(halves, (x, 1 - x)):
            rows = pl.ds(pl.multiple_of(b * d2 + bit * part, part // 2), part)
            ref.fetch([(ref.hbm, w_ref.at[rows])])
        src = direct.hbm
        left = d2 - skip
        pairs = [(src.at[:left], w_ref.at[pl.ds(pl.multiple_of(b * d2, d2) + skip, left)])]
        for row, n, side, at, k in cuts(q):
            rows = pl.ds(pl.multiple_of(b * q, q) + row, n)
            pairs.append(
                (src.at[left + at : left + at + n, k * half : (k + 1) * half], wo2.at[rows, side * half : (side + 1) * half])
            )
        direct.fetch(pairs)
    vec = ins.vec()
    fill_bias(vec, bias_ref)
    bqv = ins.other()[B_QV : B_QV + 1]
    bias = []
    for p in range(half // PAIR):
        bias += [bqv[:, p * PAIR : (p + 1) * PAIR], jnp.zeros((1, PAIR), F32)]
        bias += [bqv[:, half + p * PAIR : half + (p + 1) * PAIR]]
    n1 = ins.n1()
    for ref in (ins.mine, ins.rest, ins.r, ins.rx, ins.rc, ins.rcx):
        ref()
    out.w.send([(w_ref, out.w.hbm)])
    out.wo2.send()
    z = (mm(n1[...], w_ref[...]) + jnp.concatenate(bias, axis=1)).astype(BF)
    out.qkv.vmem[...] = z
    out.qkv.send()
    ctx2 = out.ctx2.vmem
    for p in range(half // PAIR):
        parts = (z[:, (3 * p + m) * PAIR : (3 * p + m + 1) * PAIR] for m in range(3))
        ctx2[:, p * PAIR : (p + 1) * PAIR] = attend_pair(*parts, bias_ref, out.lse.vmem, 2 * p)
    out.ctx2.send()
    out.lse.send()
    hidden = ins.tok()[...].astype(F32) + vec[B_OUT : B_OUT + 1]
    hidden = hidden + (mm(ins.ctx1()[...], ins.wo1()[...]) + mm(ctx2[...], wo2[...]))
    out.hid.vmem[...] = hidden
    out.hid.send()
    xhat, _ = norm_parts(hidden)
    n2 = (xhat * vec[GAIN2 : GAIN2 + 1] + vec[SHIFT2 : SHIFT2 + 1]).astype(BF)
    for k, ref in enumerate((out.na, out.nb)):
        ref.vmem[...] = n2[k * SEQ // 2 : (k + 1) * SEQ // 2]
        ref.send()


def feed_body(own, first, s, ins, out):
    y = s[1]
    wu_ref, wd_ref = ins.wu, ins.wd
    d = ins.na.hbm.shape[1]
    rows = out.act.vmem.shape[0]
    n2, wu, wd = ins.na.vmem, wu_ref.vmem, wd_ref.vmem
    ins.na.fetch([(ins.na.hbm, n2.at[: SEQ // 2])])
    if own:
        ins.nb.fetch([(ins.nb.hbm, n2.at[SEQ // 2 :])])
    wu_ref.fetch([(wu_ref.hbm.at[:, k * d : (k + 1) * d], wu.at[k]) for k in range(2)])
    ins.dn.fetch([(ins.dn.hbm.at[first : first + rows], ins.dn.vmem)])
    wd_ref.fetch([(wd_ref.hbm.at[k * d : (k + 1) * d], wd.at[k]) for k in range(2)])
    waits_u, waits_d = wu_ref.pending, wd_ref.pending
    vec = ins.vec()
    ins.na()
    if own:
        ins.nb()
    dn = ins.dn()
    act, gg = out.act.vmem, out.gg.vmem
    for k in range(2):
        cols = slice(k * d, (k + 1) * d)
        waits_u[k].wait()
        gate = mm(n2[...], wu[k]) + vec[pl.ds(B_UP + 2 * y + k, 1), :]
        waits_d[k].wait()
        dact = nt(dn[...], wd[k])
        cdf = 0.5 * (1.0 + lax.erf(gate * (0.5**0.5)))
        pdf = jnp.exp(gate * gate * -0.5) * 0.3989422804014327
        act[:, cols] = (gate * cdf).astype(BF)
        gg[:, cols] = (dact * (cdf + gate * pdf)).astype(BF)
    out.act.send()
    out.gg.send()
    kind = F32 if own else BF
    out.u.vmem[...] = (nt(gg[:, :d], wu[0]) + nt(gg[:, d:], wu[1])).astype(kind)
    out.u.send()
    out.o.vmem[...] = (mm(act[:, :d], wd[0]) + mm(act[:, d:], wd[1])).astype(kind)
    out.o.send()


def feed_grads_body(s, ins, out, n2, dn, act, gg):
    c = s[0]
    d = n2.shape[1]
    early = ((ins.gg1, ins.gg2, ins.gg3, gg), (ins.na, ins.nb, ins.nc, ins.nd, n2))
    late = ((ins.act1, ins.act2, ins.act3, act), (ins.dn1, ins.dn2, dn))
    for *parts, to in early + late:
        at = 0
        for ref in parts:
            rows = ref.hbm.shape[0]
            ref.fetch([(ref.hbm, to.at[at : at + rows])])
            at += rows
    hold = out.uk.hbm.shape
    n, r2 = hold[0], hold[1]
    r = r2 // 2
    for *parts, _ in early:
        for ref in parts:
            ref()
    gu, gd = out.uk.vmem, out.dk.vmem
    for k in range(2):
        cols = slice(k * d, (k + 1) * d)
        gu[k] = tn(n2[...], gg[:, cols]).astype(BF).reshape(n, 2, r, d)
        for to, b in ((out.us, 1 - c), (out.uk, c)):
            to.send([(gu.at[k, :, b], to.hbm.at[:, k * r : (k + 1) * r])])
    for *parts, _ in late:
        for ref in parts:
            ref()
    for k in range(2):
        cols = slice(k * d, (k + 1) * d)
        gd[k] = tn(act[:, cols], dn[...]).astype(BF).reshape(n // 2, 2, r2, d)
        for to, b in ((out.ds, 1 - c), (out.dk, c)):
            to.send([(gd.at[k, :, b], to.hbm.at[k * n // 2 : (k + 1) * n // 2])])
        out.gb.vmem[k : k + 1] = jnp.sum(gg[:, cols].astype(F32), axis=0, keepdims=True)


def middle_body(s, ins, out):
    vec = ins.vec()
    hidden = ins.hid()[...]
    xhat, r = norm_parts(hidden)
    e = ins.u1()[...] + jnp.concatenate((ins.ua()[...], ins.ub()[...]), axis=0).astype(F32)
    dn = ins.dn()[...].astype(F32)
    grad_hidden = dn + norm_back(e, xhat, r, vec[GAIN2 : GAIN2 + 1])
    out.gh.vmem[...] = grad_hidden
    out.gh.send()
    ag = grad_hidden.astype(BF)
    out.gc2.vmem[...] = nt(ag, ins.wo2()[...]).astype(BF)
    out.gc2.send()
    out.gc1.vmem[...] = nt(ag, ins.wo1()[...]).astype(BF)
    out.gc1.send()
    out.go2.vmem[...] = tn(ins.ctx2()[...], ag).astype(BF)
    out.go2.send()
    out.go1.vmem[...] = tn(ins.ctx1()[...], ag).astype(BF)
    out.go1.send()
    small = out.small.vmem
    small[GAIN2 : GAIN2 + 1] = jnp.sum(e * xhat, axis=0, keepdims=True)
    small[SHIFT2 : SHIFT2 + 1] = jnp.sum(e, axis=0, keepdims=True)
    small[B_OUT : B_OUT + 1] = jnp.sum(ag.astype(F32), axis=0, keepdims=True)
    small[B_DOWN : B_DOWN + 1] = jnp.sum(dn, axis=0, keepdims=True)
    out.small.send()


def attend_pair_back(q2, k2, v2, g2, bias_ref, lse_ref, at):
    lane = lax.broadcasted_iota(jnp.int32, (SEQ, PAIR), 1)
    row = lax.broadcasted_iota(jnp.int32, (PAIR, SEQ), 0)
    q2 = q2 * BF(HD**-0.5)
    kt = jnp.transpose(k2)
    dq, dk, dv = [], None, None
    for b in range(SEQ // BLOCK):
        rows = slice(b * BLOCK, (b + 1) * BLOCK)
        dqt = None
        for e in range(2):
            on = (lane[rows] // HD) == e
            qe = jnp.where(on, q2[rows], BF(0))
            ge = jnp.where(on, g2[rows], BF(0))
            ke = jnp.where((row // HD) == e, kt, BF(0))
            s = nt(k2, qe) + bias_ref[:, rows]
            probs = jnp.exp(s - lse_ref[at + e : at + e + 1, rows])
            gp = nt(v2, ge)
            delta = jnp.sum(gp * probs, axis=0, keepdims=True)
            gs = (probs * (gp - delta)).astype(BF)
            t = mm(probs.astype(BF), ge)
            dv = t if dv is None else dv + t
            t = mm(gs, qe)
            dk = t if dk is None else dk + t
            t = mm(ke, gs)
            dqt = t if dqt is None else dqt + t
        dq.append((jnp.transpose(dqt) * (HD**-0.5)).astype(BF))
    return jnp.concatenate(dq, axis=0), dk.astype(BF), dv.astype(BF)


def weight_grads(c, ins, out, gw, half):
    d2, q = gw.shape[0] // 2, half // 2
    go = ins.go()
    for dst, b in ((out.gws, 1 - c), (out.gwk, c)):
        dst.send([(gw.at[pl.ds(pl.multiple_of(b * d2, d2), d2)], dst.hbm.at[:d2])])
        for row, n, side, at, k in cuts(q):
            src = go.at[pl.ds(pl.multiple_of(b * q, q) + row, n), side * half : (side + 1) * half]
            dst.send([(src, dst.hbm.at[d2 + at : d2 + at + n, k * half : (k + 1) * half])])


def other_back_body(half, s, ins, out, bias_ref, gw):
    grad_ref = out.grad.vmem
    fill_bias(ins.vec(), bias_ref)
    for p in range(half // PAIR):
        at = [slice(m * half + p * PAIR, m * half + (p + 1) * PAIR) for m in range(3)]
        local = [slice((3 * p + m) * PAIR, (3 * p + m + 1) * PAIR) for m in range(3)]
        parts = [ins.qkv()[:, local[m]] for m in range(3)]
        grads = attend_pair_back(*parts, ins.gc()[:, at[0]], bias_ref, ins.lse(), 2 * p)
        for m in range(3):
            grad_ref[:, at[m]] = grads[m]
    out.grad.send()
    gw[...] = tn(ins.n1()[...], grad_ref[...]).astype(BF)
    weight_grads(s[0], ins, out, gw, half)


def own_back_body(half, s, ins, out, bias_ref, gw):
    grad_ref = out.grad.vmem
    fill_bias(ins.vec(), bias_ref)
    for p in range(half // PAIR):
        at = [slice(m * half + p * PAIR, m * half + (p + 1) * PAIR) for m in range(3)]
        parts = [ins.qkv()[:, at[m]] for m in range(3)]
        grads = attend_pair_back(*parts, ins.gc()[:, at[0]], bias_ref, ins.lse(), 2 * p)
        for m in range(3):
            grad_ref[:, at[m]] = grads[m]
    out.grad.send()
    gw[...] = tn(ins.n1()[...], grad_ref[...]).astype(BF)
    weight_grads(s[0], ins, out, gw, half)


def last_body(half, s, ins, out, w_ref):
    vec = ins.vec()
    y = s[1]
    mine, theirs = ins.grad1(), ins.grad2()
    e = None
    for m, w in enumerate((ins.wq, ins.wk, ins.wv)):
        t = nt(mine[:, m * half : (m + 1) * half], w()[...])
        e = t if e is None else e + t
    w = ins.w()
    for p in range(half // PAIR):
        for m in range(3):
            at = slice(m * half + p * PAIR, m * half + (p + 1) * PAIR)
            w_ref[:, at] = w[:, (3 * p + m) * PAIR : (3 * p + m + 1) * PAIR]
    e = e + nt(theirs[...], w_ref[...])
    xhat, r = norm_parts(ins.tok()[...].astype(F32))

    def put(k, row):
        for side in range(2):
            at = 2 * k + side
            columns = slice(at % 3 * half, (at % 3 + 1) * half)
            out.small.vmem[at // 3 : at // 3 + 1, columns] = row[:, side * half : (side + 1) * half]

    before = ins.small2()
    for k in (GAIN2, SHIFT2, B_OUT, B_DOWN):
        put(k, before[k : k + 1])
    put(GAIN1, jnp.sum(e * xhat, axis=0, keepdims=True))
    put(SHIFT1, jnp.sum(e, axis=0, keepdims=True))
    sums = [jnp.sum(v[...].astype(F32), axis=0, keepdims=True) for v in (mine, theirs)]
    for k in range(2):
        a, b = (v[:, 2 * k * half : (2 * k + 1) * half] for v in sums)
        both = jnp.where(y == 0, jnp.concatenate((a, b), axis=1), jnp.concatenate((b, a), axis=1))
        put(G_QV + k, both)
    gb = ins.gb()
    for k in range(4):
        row = gb[k % 2 : k % 2 + 1]
        put(G_UP + k, jnp.where(y == k // 2, row, jnp.zeros_like(row)))
    out.small.send()
    out.gt.vmem[...] = ins.gh()[...] + norm_back(e, xhat, r, vec[GAIN1 : GAIN1 + 1])
    out.gt.send()


def output_body(s, ins, out):
    bias = ins.vec()[B_DOWN : B_DOWN + 1]
    res = ins.hid()[...] + (ins.o1()[...] + ins.o2()[...].astype(F32)) + bias
    out.out.vmem[...] = res.astype(BF)
    out.out.send()


def place(s, refs, order, buf):
    for k, ref in enumerate(refs):
        core, first = s[0] ^ (k >> 1), k & 1
        pairs = []
        for m in range(4):
            at = 0
            for level, bit in zip(order, (first, m >> 1)):
                at = at + (s[2 + level] ^ bit) * (1 << (level - 1))
            at = at + (m & 1) * 4
            pairs.append((ref.hbm.at[m >> 1, m & 1], buf.at[2 * at + core]))
        ref.fetch(pairs)


def results_body(half, order_a, order_b, s, ins, out, up, down, buf):
    z = s[4] + 2 * s[5]
    n, r = buf.shape[1:3]
    refs = (ins.a, ins.b, ins.c, ins.d)
    ups, downs = (ins.u0, ins.u1, ins.u2, ins.u3), (ins.d0, ins.d1, ins.d2, ins.d3)
    place(s, ups, order_a, up)
    for k, ref in enumerate(refs):
        core, x = s[0] ^ (k >> 1), s[3] ^ (k & 1)
        ref.fetch([(ref.hbm.at[m * r : (m + 1) * r], buf.at[core, (z ^ m) * 2 + x]) for m in range(4)])
    place(s, downs, order_b, down)
    i, r2, d = up.shape
    h2 = r2 // 2
    for ref in ups:
        ref()
    to = out.gu.vmem
    for k in range(2):
        part = slice(k * i // 2, (k + 1) * i // 2)
        rows = slice(k * i * h2 // 2, (k + 1) * i * h2 // 2)
        for h in range(2):
            to[rows, h * d : (h + 1) * d] = up[part, h * h2 : (h + 1) * h2].astype(F32).reshape(i * h2 // 2, d)
        out.gu.send([(to.at[rows], out.gu.hbm.at[rows])])
    for ref in refs:
        ref()
    d2, q = half, half // 2
    for c in range(2):
        whole = buf[c].reshape(n * r, buf.shape[3])
        for m, ref in enumerate((out.gq, out.gk, out.gv)):
            ref.vmem[c * d2 : (c + 1) * d2] = whole[:d2, m * half : (m + 1) * half].astype(F32)
            ref.send([(ref.vmem.at[c * d2 : (c + 1) * d2], ref.hbm.at[c * d2 : (c + 1) * d2])])
        for row, size, side, at, k in cuts(q):
            piece = whole[d2 + at : d2 + at + size, k * half : (k + 1) * half]
            out.go.vmem[c * q + row : c * q + row + size, side * half : (side + 1) * half] = piece.astype(F32)
    out.go.send()
    for ref in downs:
        ref()
    to = out.gd.vmem
    for k in range(2):
        part = slice(k * i // 2, (k + 1) * i // 2)
        rows = slice(k * i * r2 // 2, (k + 1) * i * r2 // 2)
        to[rows] = down[part].astype(F32).reshape(i * r2 // 2, d)
        out.gd.send([(to.at[rows], out.gd.hbm.at[rows])])


def make_per_device(dp_size):
    bits = dp_size.bit_length() - 1
    assert dp_size == 1 << bits and bits >= 4
    group = 16
    levels, extra = (1, 2, 3), tuple(range(4, bits))

    def after(value, *others):
        return lax.optimization_barrier((value,) + others)[0]

    def swap(value, level, start=None, until=None):
        if start is not None:
            value = after(value, start)
        if level == "h":
            got = lax.ppermute(value, "head", [(0, 1), (1, 0)])
        else:
            got = lax.ppermute(value, "dp", [(i, i ^ (1 << level)) for i in range(dp_size)])
        return got if until is None else after(got, until)

    def after_all(values, others):
        return lax.optimization_barrier((values, others))[0]

    def tie(kernel, others):
        got, others = lax.optimization_barrier((vars(kernel), others))
        return types.SimpleNamespace(**got), others

    def my_bit(level):
        return (lax.axis_index("dp") >> level) & 1

    def plus(*terms):
        return sum(t.astype(F32) for t in terms).astype(BF)

    def swap_z(values):
        return [
            lax.ppermute(v, "dp", [(i, i ^ (m << 2)) for i in range(dp_size)])
            for m, v in zip((1, 2, 3), values)
        ]

    def cut_x(*terms):
        b = my_bit(1)
        pick = lambda t, k: lax.dynamic_index_in_dim(t, k, 1, keepdims=False)
        return plus(*(pick(t, 1 - b) for t in terms)), plus(*(pick(t, b) for t in terms))

    def cut_z(*terms):
        z = (lax.axis_index("dp") >> 2) & 3
        pick = lambda t, k: lax.dynamic_index_in_dim(t, k, 0, keepdims=False)
        return [plus(*(pick(t, z ^ m) for t in terms)) for m in (1, 2, 3, 0)]

    class Part:
        def __init__(self, *terms, cut=True):
            self.terms = [t.reshape((2, 2, 2, -1, t.shape[-1])) for t in terms] if cut else list(terms)
            self.left, self.gathering = list(levels[::-1]), False

        def wait(self, until):
            self.terms[-1] = after(self.terms[-1], until)

        def step(self, level, until=None):
            axis = self.left.index(level)
            self.left.remove(level)
            b = my_bit(level)
            pick = lambda t, k: lax.dynamic_index_in_dim(t, k, axis, keepdims=False)
            sent = plus(*(pick(t, 1 - b) for t in self.terms))
            kept = plus(*(pick(t, b) for t in self.terms))
            self.terms = [kept, swap(sent, level, until=until)]
            return sent

        def widen(self, level):
            mine = self.value()
            self.terms = [mine, swap(mine, level)]

        def value(self):
            if self.gathering and len(self.terms) > 1:
                self.terms = [jnp.stack(self.terms)]
            if len(self.terms) > 1:
                self.terms = [plus(*self.terms)]
            return self.terms[0]

    def per_device(
        tokens, segments, padding, cotangent, gain_one, shift_one, w_query, b_query, w_key,
        w_value, b_value, w_out, b_out, gain_two, shift_two, w_up, b_up, w_down, b_down,
    ):
        rows, d = tokens.shape
        assert rows == SEQ
        y, dp = lax.axis_index("head"), lax.axis_index("dp")
        half, hid = w_query.shape[1], w_up.shape[1]
        rows_c = d // 2 + half // 3
        r = d // group
        scalars = jnp.stack((dp & 1, y, dp, (dp >> 1) & 1, (dp >> 2) & 1, (dp >> 3) & 1))
        scalars = scalars.astype(jnp.int32)
        line = lambda v: jnp.pad(
            lax.dynamic_slice_in_dim(v, y * rows, rows).astype(F32), (0, d - rows)
        )
        vec = jnp.concatenate(
            (gain_one, shift_one, b_out, gain_two, shift_two, b_down, b_query, b_value,
             line(segments), line(padding), b_up, jnp.zeros((VEC_ROWS * d - 9 * d - 2 * hid,), F32))
        ).reshape(VEC_ROWS, d)
        square = pltpu.VMEM((SEQ, SEQ), F32)
        act, wide, part = ((SEQ, d), BF), ((SEQ, d), F32), ((SEQ, half), BF)
        three = ((SEQ, 3 * half), BF)
        lse = ((8, SEQ), F32)
        rows_half = ((SEQ // 2, d), BF)

        relayed = 320
        sent = call(
            functools.partial(pack_body, d, half, relayed), scalars,
            dict(wq=Manual(w_query), wk=Manual(w_key), wv=Manual(w_value), wo=Manual(w_out)),
            dict(r=Stored(((relayed // 2, 3 * half), BF), (8, 128)),
                 p=Stored(((rows_c - relayed, 3 * half), BF), (8, 128))),
            scratch=[pltpu.VMEM((rows_c, 3 * half), BF)],
        )
        one = call(
            functools.partial(first_body, half), scalars,
            dict(vec=Free(vec), tok=Lazy(tokens), wq=Lazy(w_query), wk=Lazy(w_key), wv=Lazy(w_value),
                 cot=Lazy(cotangent)),
            dict(n1=Stored(act), qkv=Stored(three), ctx=Stored(part), lse=Stored(lse), dn=Stored(act),
                 vec=((VEC_ROWS, d), F32)),
            scratch=[square], micros=8,
        )
        one, relay = tie(one, swap(sent.r, "h"))
        n1, dn = one.n1, one.dn
        relay_x, mine, other = swap(relay, 1), swap(sent.p, "h"), swap(vec, "h")
        vec = one.vec
        relay_c = swap(relay, 0)
        relay_x, mine, other = lax.optimization_barrier((relay_x, mine, other))
        dn_oth = swap(dn, "h", start=mine)
        weights = dict(mine=Manual(mine), rest=Manual(swap(mine, 0)), r=Manual(relay), rx=Manual(relay_x),
                       rc=Manual(relay_c), rcx=Manual(swap(relay_x, 0)))
        two = call(
            functools.partial(second_body, half), scalars,
            dict(vec=vec, other=Free(other), n1=Lazy(n1), tok=Lazy(tokens), ctx1=Lazy(one.ctx),
                 wo1=Lazy(w_out), **weights),
            dict(w=Stored(((d, 3 * half), BF), (16, 128)), qkv=Stored(three), lse=Stored(lse),
                 wo2=Stored(((half, d), BF)), ctx2=Stored(part), hid=Stored(wide), na=Stored(rows_half), nb=Stored(rows_half)),
            scratch=[square, pltpu.VMEM((d, 3 * half), BF)], micros=12,
        )
        two, dn_oth = tie(two, dn_oth)

        na, nb = swap(two.na, "h"), swap(two.nb, "h")

        def feed(first, dn, **rows):
            own = first is None
            count = SEQ if own else SEQ // 2
            units = Stored(((count, hid), BF))
            partial = Stored(((count, d), F32 if own else BF))
            at = {k: Manual(v, None if i else (count, d)) for i, (k, v) in enumerate(rows.items())}
            return call(
                functools.partial(feed_body, own, first or 0), scalars,
                dict(vec=vec, dn=Manual(dn, (count, d)), wu=Manual(w_up, (2, d, d)),
                     wd=Manual(w_down, (2, d, d)), **at),
                dict(act=units, gg=units, u=partial, o=partial),
                micros=8,
            )

        f1, na = tie(feed(None, dn, na=two.na, nb=two.nb), na)
        f2 = feed(0, dn_oth, na=na)
        u_a = swap(f2.u, "h")
        f2, nb = tie(f2, nb)
        f3 = feed(SEQ // 2, dn_oth, na=nb)
        f3, u_a = tie(f3, u_a)
        u_b = swap(f3.u, "h")
        eighth = ((group // 2, 2 * r, d), BF)
        fg = call(
            feed_grads_body, scalars,
            dict(gg1=Manual(f1.gg), gg2=Manual(f2.gg), gg3=Manual(f3.gg), na=Manual(two.na), nb=Manual(two.nb),
                 nc=Manual(na), nd=Manual(nb), act1=Manual(f1.act), act2=Manual(f2.act), act3=Manual(f3.act),
                 dn1=Manual(dn), dn2=Manual(dn_oth)),
            dict(us=Stored(eighth, (8, 128)), uk=Stored(eighth, (2, group // 2, 2, r, d)),
                 ds=Stored(eighth, (8, 128)), dk=Stored(eighth, (2, group // 4, 2, 2 * r, d)),
                 gb=((8, d), F32)),
            scratch=[pltpu.VMEM((2 * SEQ, d), BF)] * 2 + [pltpu.VMEM((2 * SEQ, hid), BF)] * 2,
            micros=8,
        )
        fg, u_b = tie(fg, u_b)
        fg, u_b = tie(fg, u_b)
        up = Part(fg.uk, swap(fg.us, 0))
        down = Part(fg.dk, swap(fg.ds, 0))
        first_sent = up.step(1), down.step(2)

        mid = call(
            middle_body, scalars,
            dict(vec=vec, hid=two.hid, u1=f1.u, ua=Lazy(u_a), ub=Lazy(after(u_b, *first_sent)), dn=dn,
                 wo2=two.wo2, wo1=w_out, ctx2=two.ctx2, ctx1=one.ctx),
            dict(gh=Stored(wide), gc2=part, gc1=Stored(part), go2=Stored(((half, d), BF)),
                 go1=Stored(((half, d), BF)), small=((8, d), F32)),
            micros=6,
        )
        mid, (up.terms[-1], down.terms[-1]) = tie(mid, (up.terms[-1], down.terms[-1]))
        second_sent = up.step(2), down.step(1)
        piece = ((rows_c, 3 * half), BF)
        back = dict(
            outs=dict(gws=Stored(piece, (16, 128)), gwk=Stored(piece, (16, 128)), grad=Stored(three)),
            scratch=[square, pltpu.VMEM((d, 3 * half), BF)],
            micros=11,
        )
        o_oth = swap(jnp.concatenate((f2.o, f3.o)), "h", start=mid.gc2)
        b2 = call(
            functools.partial(other_back_body, half), scalars,
            dict(vec=vec, gc=after(mid.gc2, *second_sent), go=Lazy(mid.go2), n1=n1, qkv=two.qkv, lse=two.lse),
            **back,
        )
        b2, (up.terms[-1], down.terms[-1]) = tie(b2, (up.terms[-1], down.terms[-1]))
        grid = lambda v: v.reshape((4, 2, -1, v.shape[-1]))
        oth_sent, oth_kept = cut_x(grid(b2.gwk), grid(swap(b2.gws, 0)))
        ab = plus(*up.terms), plus(*down.terms)
        ab_got = swap(ab[0], 3), swap(ab[1], 3)
        third_sent = *ab, oth_sent
        oth_got = swap(oth_sent, 1)
        b1 = call(
            functools.partial(own_back_body, half), scalars,
            dict(vec=vec, gc=Lazy(mid.gc1), go=Lazy(mid.go1), qkv=Lazy(after(one.qkv, *third_sent)),
                 lse=one.lse, n1=n1),
            **back,
        )
        b1, (oth_got, up_got, o_oth) = tie(b1, (oth_got, ab_got[0], o_oth))
        theirs = plus(oth_kept, oth_got)
        own_c = after_all(swap(b1.gws, 0), theirs)
        theirs = swap(theirs, "h")
        own_sent, own_kept = cut_x(grid(b1.gwk), grid(own_c))
        own_got = swap(own_sent, 1)
        last_sent = (own_sent,)
        last = call(
            functools.partial(last_body, half), scalars,
            dict(vec=vec, grad1=Lazy(after(b1.grad, *last_sent)), grad2=Lazy(b2.grad), wq=w_query,
                 wk=w_key, wv=w_value, tok=tokens, gh=Lazy(mid.gh), small2=mid.small,
                 gb=fg.gb, w=two.w),
            dict(small=((SUM_ROWS, 3 * half), F32), gt=Stored(wide)),
            scratch=[pltpu.VMEM((d, 3 * half), BF)], micros=12,
        )
        last, (own_got, theirs, down_got) = tie(last, (own_got, theirs, ab_got[1]))
        *own_sent, own_kept = cut_z(own_kept, own_got, theirs)
        own_z = swap_z(own_sent)
        ab, ab_got = after_all((ab, (up_got, down_got)), own_sent)
        feed_sums = [plus(p, q) for p, q in zip(ab, ab_got)]
        for level in extra:
            feed_sums = [plus(p, swap(p, level)) for p in feed_sums]
        up, down = (Part(p, cut=False) for p in feed_sums)
        up.gathering = down.gathering = True
        up.widen(1)
        down.widen(2)
        small = after_all(last.small, own_z[0])
        small = small + swap(small, 0)
        small = small + swap(small, "h")
        output = call(
            output_body, scalars,
            dict(vec=vec, hid=Lazy(after_all(two.hid, feed_sums)), o1=Lazy(f1.o), o2=Lazy(o_oth)),
            dict(out=Stored(act)), micros=4,
        )
        output, own_z = tie(output, own_z)
        n = rows_c // 8
        total = plus(own_kept, *own_z)
        for level in extra:
            total = plus(total, swap(total, level))
            small = small + swap(small, level)
        message = jnp.concatenate((total, small.astype(BF)))
        got = swap_z([message] * 3)
        up.terms[-1], down.terms[-1] = after_all((up.terms[-1], down.terms[-1]), message)
        u, d_ = up.value(), down.value()
        u_got, d_got, u_c, d_c = swap(u, 2), swap(d_, 1), swap(u, 0), swap(d_, 0)
        got, u_c, d_c = after_all((got, u_c, d_c), (u, d_))
        small = small + sum(g[n:].astype(F32) for g in got)
        w_all = jnp.concatenate([total] + [g[:n] for g in got] + [small.astype(BF)])
        w_x, w_c = swap(w_all, 1), swap(w_all, 0)
        u_got, d_got = after_all((u_got, d_got), w_all)
        u_got, d_got = after_all((u_got, d_got), w_all)
        w_x, u_cx, d_cx = lax.optimization_barrier((w_x, swap(u_got, 0), swap(d_got, 0)))
        block = Stored(((d, half), F32))
        done = call(
            functools.partial(results_body, half, (2, 1), (1, 2)), scalars,
            dict(u0=Manual(u), u1=Manual(u_got), u2=Manual(u_c), u3=Manual(u_cx),
                 d0=Manual(d_), d1=Manual(d_got), d2=Manual(d_c), d3=Manual(d_cx),
                 a=Manual(w_all), b=Manual(w_x), c=Manual(w_c), d=Manual(swap(w_x, 0))),
            dict(gu=Stored(((d, hid), F32)), gd=Stored(((hid, d), F32)), gq=block, gk=block, gv=block,
                 go=Stored(((half, d), F32))),
            scratch=[pltpu.VMEM((group, 2 * r, d), BF)] * 2 + [pltpu.VMEM((2, 8, n, 3 * half), BF)], micros=9,
        )
        own_bias = lambda v: lax.dynamic_slice_in_dim(v, y * half, half)
        small = (small + w_x[4 * n :].astype(F32)).reshape(-1)
        vectors = [small[k * d : (k + 1) * d] for k in (GAIN1, SHIFT1, B_OUT, GAIN2, SHIFT2, B_DOWN)]
        vectors += [own_bias(small[k * d : (k + 1) * d]) for k in (G_QV, G_QV + 1)]
        vectors.append(small[G_UP * d : (G_UP + 4) * d])
        gain1, shift1, bo, gain2, shift2, bd, bq, bv, bu = vectors
        return (
            output.out, last.gt, gain1, shift1, done.gq, bq, done.gk, done.gv, bv, done.go,
            bo, gain2, shift2, done.gu, bu, done.gd, bd,
        )

    return per_device


def solution(mesh):
    rows, heads = P(("dp", "head"), None), P("head")
    columns, lines = P(None, "head"), P("head", None)
    in_specs = (
        rows, P("dp"), P("dp"), rows, P(), P(), columns, heads, columns, columns, heads,
        lines, P(), P(), P(), columns, P(), lines, P(),
    )
    out_specs = (
        rows, rows, P(), P(), columns, heads, columns, columns, heads, lines, P(), P(), P(),
        columns, P(), lines, P(),
    )
    return jax.shard_map(
        make_per_device(mesh.shape["dp"]),
        mesh=mesh,
        in_specs=in_specs,
        out_specs=out_specs,
        check_vma=False,
    )
```
